512 devices in a mesh: dom: 128 (over z_hi, x, y), edge: 4 (over z_lo, core).
Axes of the slice: x: 4, y: 8, z: 8 (z_hi: 4, z_lo: 2; z = z_hi * 2 + z_lo), core: 2. Of those that a mesh axis runs over, the one named last changes fastest.
Arguments:
- embeddings: float32 [400, 65536], P(None, 'dom'), may hold values from -1.2 to 1.2
- accum: float32 [65536], P('dom'), may hold values from 0.01 to 1
- relations: float32 [400, 1024], replicated, may hold values from -6 to 6
- rel_accum: float32 [1024], replicated, may hold values from 0.01 to 1
- src_ids: int32 [128, 4096], P('dom', 'edge'), may hold values from 0 to 511
- rel_ids: int32 [128, 4096], P('dom', 'edge'), may hold values from 0 to 1023
- dst_ids: int32 [128, 4096], P('dom', 'edge'), may hold values from 0 to 511
- neg_ids: int32 [128, 8, 1024], P('dom', 'edge'), may hold values from 0 to 511
- bucket_len: int32 [128], P('dom'), may hold values from 512 to 4096, as said below
- partner: int32 [128], replicated, may hold values from 0 to 127, as said below
Outputs:
- new_embeddings: float32 [400, 65536], P(None, 'dom')
- new_accum: float32 [65536], P('dom')
- new_relations: float32 [400, 1024], replicated
- new_rel_accum: float32 [1024], replicated
The draws below stay inside these ranges and needn't reach their ends.
Inputs may be any that keep to these rules, and one draw needn't show every extreme that they name: The live slots of bucket d are its first bucket_len[d] slots; some bucket is full in every draw. partner[partner[d]] == d and partner[d] != d for every d.
All inputs are finite; a program needn't handle non-finite values.
Results may differ from the reference program's by a relative error of at most 0.0003.
The reference program's roundings to bfloat16 on the way count: a program that leaves them out, or rounds other values in their place, can miss the bound.
Values may be sent and summed in bfloat16 or wider, within the bound.
A program may use at most 64 MiB of HBM per device.

```python
import math
import jax
import jax.numpy as jnp
from jax import lax

DIM = 400
ENT_DOM = 512
NEG = 1024
REL = 1024
BLOCKS_DEV = 2
BUCKET_EDGES = 4096
ENTITIES = 65536
N_DOM = 128
N_EDGE = 4


def draw_bucket_len(key, part):
    key = jax.random.fold_in(key, 11)
    first, second = jax.random.split(key)
    count = ENTITIES // ENT_DOM
    spread = jax.random.randint(first, (count,), BUCKET_EDGES // 8, BUCKET_EDGES + 1, dtype=jnp.int32)
    chosen = jax.random.randint(second, (), 0, count, dtype=jnp.int32)
    return jnp.where(jnp.arange(count, dtype=jnp.int32) == chosen, BUCKET_EDGES, spread).astype(jnp.int32)


def draw_partner(key, part):
    key = jax.random.fold_in(key, 23)
    count = ENTITIES // ENT_DOM
    order = jax.random.permutation(key, jnp.arange(count, dtype=jnp.int32))
    evens = order[0::2]
    odds = order[1::2]
    paired = jnp.zeros((count,), jnp.int32).at[evens].set(odds).at[odds].set(evens)
    return paired


def place_ends(array, key, least, largest):
    longest = array.shape.index(max(array.shape))
    spots = []
    for shift in (0, 1):
        where = [jax.random.randint(jax.random.fold_in(key, axis), (), 0, length) for axis, length in enumerate(array.shape)]
        where[longest] = (where[longest] + shift) % array.shape[longest]
        spots.append(tuple(where))
    return array.at[spots[0]].set(least).at[spots[1]].set(largest)


def block_scale(stream_key, dims, pieces, least, largest):
    level, own = 1.0, jax.random.fold_in(stream_key, 6)
    for dim, parts in pieces:
        heights = jnp.exp(jax.random.uniform(jax.random.fold_in(own, dim), (parts,), jnp.float32, least / len(pieces), largest / len(pieces)))
        level = level * jnp.repeat(heights, dims[dim] // parts).reshape([-1 if axis == dim else 1 for axis in range(len(dims))])
    return level


def centred(own_key, extent, scale, most, shards=(), kind=jnp.bfloat16):
    result = scale * jax.random.normal(own_key, extent, jnp.float32)
    if shards:
        result = result * block_scale(own_key, extent, shards, -0.22, 0.18)
    return jnp.clip(result, -most, most).astype(kind)


def setup_inputs(seed: int = 0) -> dict:
    streams_of = jax.random.split(jax.random.key(seed), 11)
    embeddings = centred(streams_of[0], (DIM, ENTITIES), 0.2, 1.2, ((1, 128),), jnp.float32)
    accum = jnp.clip(jnp.exp(math.log(1.0) - 4.6051702 * jax.random.uniform(streams_of[1], (ENTITIES,), jnp.float32) ** block_scale(streams_of[1], (ENTITIES,), ((0, 128),), -0.2, 0.2)), 0.01, 1.0)
    relations = centred(streams_of[2], (DIM, REL), 1.0, 6.0, (), jnp.float32)
    rel_accum = jnp.clip(jnp.exp(jax.random.uniform(streams_of[3], (REL,), jnp.float32, math.log(0.01), math.log(1.0))), 0.01, 1.0)
    src_ids = place_ends(jax.random.randint(streams_of[4], (N_DOM, BUCKET_EDGES), 0, ENT_DOM), jax.random.fold_in(streams_of[4], 1), 0, ENT_DOM - 1).astype(jnp.int32)
    rel_ids = place_ends(jax.random.randint(streams_of[5], (N_DOM, BUCKET_EDGES), 0, REL), jax.random.fold_in(streams_of[5], 1), 0, REL - 1).astype(jnp.int32)
    dst_ids = place_ends(jax.random.randint(streams_of[6], (N_DOM, BUCKET_EDGES), 0, ENT_DOM), jax.random.fold_in(streams_of[6], 1), 0, ENT_DOM - 1).astype(jnp.int32)
    neg_ids = place_ends(jax.random.randint(streams_of[7], (N_DOM, N_EDGE * BLOCKS_DEV, NEG), 0, ENT_DOM), jax.random.fold_in(streams_of[7], 1), 0, ENT_DOM - 1).astype(jnp.int32)
    bucket_len = draw_bucket_len(jax.random.fold_in(streams_of[10], 71), 0)
    partner = draw_partner(jax.random.fold_in(streams_of[10], 71), 0)
    return {"embeddings": embeddings, "accum": accum, "relations": relations, "rel_accum": rel_accum, "src_ids": src_ids, "rel_ids": rel_ids, "dst_ids": dst_ids, "neg_ids": neg_ids, "bucket_len": bucket_len, "partner": partner}


learn_rate = 0.1

def bucket_terms(own_b, other_b, relations, src, rel, dst, neg, live):
    dim = own_b.shape[0]
    half = dim // 2
    edges = src.shape[0]
    blocks, negcount = neg.shape
    width = edges // blocks
    h = jnp.take(own_b, src, axis=1).astype(jnp.float32)
    t = jnp.take(other_b, dst, axis=1).astype(jnp.float32)
    r = jnp.take(relations, rel, axis=1)
    h_re, h_im = (h[:half], h[half:])
    r_re, r_im = (r[:half], r[half:])
    q = jnp.concatenate([h_re * r_re - h_im * r_im, h_re * r_im + h_im * r_re], axis=0)
    pos = lax.optimization_barrier(jnp.sum(q * t, axis=0))
    q_b = q.astype(jnp.bfloat16)
    neg_flat = neg.reshape(-1)
    neg_cols = jnp.take(other_b, neg_flat, axis=1).reshape(dim, blocks, negcount)
    q_blocks = q_b.reshape(dim, blocks, width)
    negs = jnp.einsum('dkb,dkn->kbn', q_blocks.astype(jnp.float32), neg_cols.astype(jnp.float32))
    live_blocks = live.reshape(blocks, width)
    g_pos = -live * jax.nn.sigmoid(-pos)
    g_neg = (live_blocks[:, :, None] * jax.nn.sigmoid(negs) / negcount ** 0.5).astype(jnp.bfloat16)
    back = jnp.einsum('dkn,kbn->dkb', neg_cols.astype(jnp.float32), g_neg.astype(jnp.float32)).reshape(dim, edges)
    dq = t * g_pos + back
    dt = q * g_pos
    dn = jnp.einsum('dkb,kbn->dkn', q_blocks.astype(jnp.float32), g_neg.astype(jnp.float32)).reshape(dim, blocks * negcount)
    dq_re, dq_im = (dq[:half], dq[half:])
    dh = jnp.concatenate([dq_re * r_re + dq_im * r_im, dq_im * r_re - dq_re * r_im], axis=0)
    dr = jnp.concatenate([dq_re * h_re + dq_im * h_im, dq_im * h_re - dq_re * h_im], axis=0)
    ent = own_b.shape[1]
    g_own = jnp.zeros((dim, ent), jnp.float32).at[:, src].add(dh)
    g_other = jnp.zeros((dim, ent), jnp.float32).at[:, dst].add(dt).at[:, neg_flat].add(dn)
    g_rel = jnp.zeros(relations.shape, jnp.float32).at[:, rel].add(dr)
    return (g_own, g_other, g_rel)

def reference(embeddings, accum, relations, rel_accum, src_ids, rel_ids, dst_ids, neg_ids, bucket_len, partner):
    count = partner.shape[0]
    dim = embeddings.shape[0]
    groups = embeddings.astype(jnp.bfloat16).reshape(dim, count, ENT_DOM).transpose(1, 0, 2)
    slots = jnp.arange(BUCKET_EDGES, dtype=jnp.int32)

    def one(index):
        own_b = groups[index]
        other_b = groups[partner[index]]
        live = (slots < bucket_len[index]).astype(jnp.float32)
        return bucket_terms(own_b, other_b, relations, src_ids[index], rel_ids[index], dst_ids[index], neg_ids[index], live)
    g_own, g_other, g_rel = lax.map(one, jnp.arange(count, dtype=jnp.int32))
    total = g_own + jnp.take(g_other, partner, axis=0)
    grad = total.transpose(1, 0, 2).reshape(dim, count * ENT_DOM)
    rel_grad = lax.optimization_barrier(jnp.sum(g_rel, axis=0))
    new_accum = accum + lax.optimization_barrier(jnp.mean(grad * grad, axis=0))
    new_embeddings = embeddings - learn_rate * grad / jnp.sqrt(new_accum)
    new_rel_accum = rel_accum + lax.optimization_barrier(jnp.mean(rel_grad * rel_grad, axis=0))
    new_relations = relations - learn_rate * rel_grad / jnp.sqrt(new_rel_accum)
    return (new_embeddings, new_accum, new_relations, new_rel_accum)
```

```python
import functools

import jax
import jax.numpy as jnp
from jax import lax
from jax.experimental import pallas as pl
from jax.experimental.pallas import tpu as pltpu
from jax.sharding import PartitionSpec as P

MESH = pl.DeviceIdType.MESH
VMEM = pl.BlockSpec(memory_space=pltpu.VMEM)
SMEM = pl.BlockSpec(memory_space=pltpu.SMEM)
f32, bf16, i32 = jnp.float32, jnp.bfloat16, jnp.int32
learn_rate = 0.1
DOM = 128
HUBS = 32
ID_TILES = 5


def remote(src, dst, send, recv, device):
    return pltpu.make_async_remote_copy(
        src_ref=src, dst_ref=dst, send_sem=send, recv_sem=recv, device_id=device, device_id_type=MESH
    )


def drain(ref, sem):
    pltpu.make_async_copy(ref, ref, sem).wait()


def greet(barrier, device):
    pl.semaphore_signal(barrier, inc=1, device_id=device, device_id_type=MESH)


def relay_kernel(
    ids_ref, emb_ref, len_ref, partner_ref, cols_ref, pids_ref,
    pay, hub, stage, got, send1, recv1, gsend, grecv, send2, recv2, asend, arecv,
):
    d, m = lax.axis_index("dom"), lax.axis_index("edge")
    zl, c = m // 2, m % 2
    far, near = (d, (1 - zl) * 2 + c), (d, zl * 2 + 1 - c)
    far_m, near_m = (1 - zl) * 2 + c, zl * 2 + 1 - c
    spoke_m = (d + 3) % 4
    barrier = pltpu.get_barrier_semaphore()

    def hello(j, _):
        greet(barrier, (4 * j + m, spoke_m))
        return 0

    greet(barrier, far)
    greet(barrier, near)
    lax.fori_loop(0, HUBS, hello, 0)

    mine = pl.ds(pl.multiple_of(m * 128, 128), 128)
    pay[0:25] = emb_ref[:, mine].astype(bf16).reshape(25, 16, 128)
    slot = m * 1024 + lax.broadcasted_iota(i32, (8, 128), 0) * 128 + lax.broadcasted_iota(i32, (8, 128), 1)
    for a in range(ID_TILES):
        v = ids_ref[8 * a : 8 * a + 8]
        if a == 0:
            v = jnp.where(slot < len_ref[0], v, 512)
        pay[25 + a] = jnp.concatenate([(v >> 5).astype(f32), (v & 31).astype(f32)], axis=0).astype(bf16)
    pay[30:32] = jnp.zeros((2, 16, 128), bf16)
    pl.semaphore_wait(barrier, HUBS + 2)

    def leg1(i, _):
        remote(pay.at[i], hub.at[d % 4, d // 4], send1, recv1, (4 * i + (m + 1) % 4, d % 4)).start()
        return 0

    lax.fori_loop(0, HUBS, leg1, 0)
    drain(hub.at[m], recv1)
    g_far = remote(hub.at[m], hub.at[m], gsend.at[0], grecv.at[0], far)
    g_near = remote(hub.at[m], hub.at[m], gsend.at[1], grecv.at[1], near)
    g_far.start()
    g_near.start()
    g_far.wait_recv()
    g_fwd = remote(hub.at[far_m], hub.at[far_m], gsend.at[2], grecv.at[2], near)
    g_fwd.start()
    g_near.wait_recv()
    g_fwd.wait_recv()

    def leg2(j, _):
        t = 4 * j + m
        p = partner_ref[t]
        stage[j] = hub[p % 4, p // 4]
        remote(stage.at[j], got.at[d // 4], send2, recv2, (t, spoke_m)).start()
        return 0

    lax.fori_loop(0, HUBS, leg2, 0)
    drain(got, recv2)
    block = got.at[pl.ds(0, 25)]
    a_far = remote(block, cols_ref.at[m], asend.at[0], arecv.at[0], far)
    a_near = remote(block, cols_ref.at[m], asend.at[1], arecv.at[1], near)
    a_far.start()
    a_near.start()
    cols_ref[m] = got[0:25]
    for a in range(ID_TILES):
        v = got[25 + a].astype(f32)
        pids_ref[8 * a : 8 * a + 8] = (v[:8] * 32.0 + v[8:]).astype(i32)
    a_far.wait_recv()
    a_fwd = remote(cols_ref.at[far_m], cols_ref.at[far_m], asend.at[2], arecv.at[2], near)
    a_fwd.start()
    a_near.wait_recv()
    a_fwd.wait_recv()
    for copy in (g_far, g_near, g_fwd, a_far, a_near, a_fwd):
        copy.wait_send()
    drain(pay, send1)
    drain(stage, send2)


def relay(ids, emb, length, partner):
    tile = lambda *lead: pltpu.VMEM((*lead, 16, 128), bf16)
    dma = pltpu.SemaphoreType.DMA
    return pl.pallas_call(
        relay_kernel,
        out_shape=(jax.ShapeDtypeStruct((4, 25, 16, 128), bf16), jax.ShapeDtypeStruct((40, 128), i32)),
        in_specs=[VMEM, VMEM, SMEM, SMEM],
        out_specs=(VMEM, VMEM),
        scratch_shapes=[
            tile(32), tile(4, 32), tile(32), tile(32),
            dma, dma, dma((3,)), dma((3,)), dma, dma, dma((3,)), dma((3,)),
        ],
        compiler_params=pltpu.CompilerParams(
            collective_id=1, has_side_effects=True, vmem_limit_bytes=40 * 2**20
        ),
        name="relay",
    )(ids, emb, length, partner)


def onehots(out, ids, first, rows, lanes):
    for j in range(lanes // 128):
        row = ids[pl.ds(first + j, 1), :]
        hit = lax.broadcasted_iota(i32, (rows, 128), 0) == row
        out[:, 128 * j : 128 * (j + 1)] = jnp.where(hit, 1.0, 0.0).astype(bf16)


def split3(x):
    hi = x.astype(bf16)
    rest = x - hi.astype(f32)
    mid = rest.astype(bf16)
    lo = (rest - mid.astype(f32)).astype(bf16)
    return hi, mid, lo


def dot(a, b, ca=1, cb=0):
    return lax.dot_general(a, b, (((ca,), (cb,)), ((), ())), preferred_element_type=f32)


def add3(x):
    return x[0:400] + x[400:800] + x[800:1200]


def counts(ids, first):
    total = jnp.zeros((512, 128), f32)
    for j in range(8):
        hit = lax.broadcasted_iota(i32, (512, 128), 0) == ids[pl.ds(first + j, 1), :]
        total = total + jnp.where(hit, 1.0, 0.0)
    return dot(jnp.ones((8, 128), bf16), total.astype(bf16), 1, 1)[0:1]


def complex_product(a, b):
    return jnp.concatenate(
        [a[:200] * b[:200] - a[200:] * b[200:], a[:200] * b[200:] + a[200:] * b[:200]], axis=0
    )


def conj_product(a, b):
    return jnp.concatenate(
        [a[:200] * b[:200] + a[200:] * b[200:], a[200:] * b[:200] - a[:200] * b[200:]], axis=0
    )


def compute_kernel(
    emb_ref, cols_ref, rel_ref, ids_ref, pids_ref, grel_ref, grad_ref,
    own_b, other_b, rel3, oh_src, oh_dst, oh_rel, parts, dr3, gt, dnacc,
):
    own_b[...] = emb_ref[...].astype(bf16)
    for m in range(4):
        other_b[:, 128 * m : 128 * (m + 1)] = cols_ref[m].reshape(400, 128)
    hi, mid, lo = split3(rel_ref[...])
    rel3[0:400], rel3[400:800], rel3[800:1200] = hi, mid, lo

    def bucket(ids, h_from, t_from, k, own):
        lanes = pl.ds(pl.multiple_of(k * 512, 512), 512)
        onehots(oh_src.at[:, lanes] if own else oh_src.at[:, pl.ds(0, 512)], ids, 4 * k, 512, 512)
        onehots(oh_dst.at[:, pl.ds(0, 512)] if own else oh_dst.at[:, lanes], ids, 16 + 4 * k, 512, 512)
        onehots(oh_rel.at[:, lanes], ids, 8 + 4 * k, 1024, 512)
        src = oh_src[:, lanes] if own else oh_src[:, 0:512]
        dst = oh_dst[:, 0:512] if own else oh_dst[:, lanes]
        h = dot(h_from[...], src)
        t = dot(t_from[...], dst)
        r = add3(dot(rel3[...], oh_rel[:, lanes]))
        q = complex_product(h, r)
        g_pos = -jax.nn.sigmoid(-jnp.sum(q * t, axis=0, keepdims=True))
        q_b = q.astype(bf16)
        negs = dot(t_from[...], q_b, 0, 0)
        gt[...] = (jax.nn.sigmoid(negs) * 0.03125).astype(bf16)
        return h, t, r, q, q_b, g_pos

    def own_block(k, _):
        lanes = pl.ds(pl.multiple_of(k * 512, 512), 512)
        h, t, r, q, q_b, g_pos = bucket(ids_ref, own_b, other_b, k, True)
        weighted = other_b[...].astype(f32) * counts(ids_ref, 24 + 8 * k)
        w_hi = weighted.astype(bf16)
        w_lo = (weighted - w_hi.astype(f32)).astype(bf16)
        dq = t * g_pos + dot(w_hi, gt[...]) + dot(w_lo, gt[...])
        for i, x in enumerate(split3(conj_product(dq, r))):
            parts[400 * i : 400 * (i + 1), lanes] = x
        for i, x in enumerate(split3(conj_product(dq, h))):
            dr3[400 * i : 400 * (i + 1), lanes] = x
        return 0

    lax.fori_loop(0, 2, own_block, 0)

    def rel_scatter(n, _):
        g = add3(dot(dr3[...], oh_rel[pl.ds(pl.multiple_of(n * 256, 256), 256), :], 1, 1))
        for j in range(2):
            grel_ref[:, 2 * n + j] = g[:, 128 * j : 128 * (j + 1)].reshape(50, 8, 128)
        return 0

    lax.fori_loop(0, 4, rel_scatter, 0)

    def ent_scatter(oh):
        def body(n, _):
            g = add3(dot(parts[...], oh[pl.ds(pl.multiple_of(n * 256, 256), 256), :], 1, 1))
            for j in range(2):
                grad_ref[2 * n + j] = grad_ref[2 * n + j] + g[:, 128 * j : 128 * (j + 1)].reshape(50, 8, 128)
            return 0

        lax.fori_loop(0, 2, body, 0)

    grad_ref[...] = jnp.zeros(grad_ref.shape, f32)
    ent_scatter(oh_src)

    dnacc[...] = jnp.zeros(dnacc.shape, f32)

    def partner_block(k, _):
        lanes = pl.ds(pl.multiple_of(k * 512, 512), 512)
        h, t, r, q, q_b, g_pos = bucket(pids_ref, other_b, own_b, k, False)
        for i, x in enumerate(split3(q * g_pos)):
            parts[400 * i : 400 * (i + 1), lanes] = x
        dnacc[...] = dnacc[...] + dot(q_b, gt[...], 1, 1) * counts(pids_ref, 24 + 8 * k)
        return 0

    lax.fori_loop(0, 2, partner_block, 0)
    ent_scatter(oh_dst)
    for m in range(4):
        grad_ref[m] = grad_ref[m] + dnacc[:, 128 * m : 128 * (m + 1)].reshape(50, 8, 128)


def compute(emb, cols, relations, ids, pids):
    return pl.pallas_call(
        compute_kernel,
        out_shape=(jax.ShapeDtypeStruct((50, 8, 8, 128), f32), jax.ShapeDtypeStruct((4, 50, 8, 128), f32)),
        in_specs=[VMEM] * 5,
        out_specs=(VMEM, VMEM),
        scratch_shapes=[
            pltpu.VMEM((400, 512), bf16), pltpu.VMEM((400, 512), bf16), pltpu.VMEM((1200, 1024), bf16),
            pltpu.VMEM((512, 1024), bf16), pltpu.VMEM((512, 1024), bf16), pltpu.VMEM((1024, 1024), bf16),
            pltpu.VMEM((1200, 1024), bf16), pltpu.VMEM((1200, 1024), bf16),
            pltpu.VMEM((512, 512), bf16), pltpu.VMEM((400, 512), f32),
        ],
        compiler_params=pltpu.CompilerParams(vmem_limit_bytes=56 * 2**20),
        name="bucket_grads",
    )(emb, cols, relations, ids, pids)


def reduce_kernel(
    grel_ref, grad_ref, emb_ref, acc_ref, rel_ref, racc_ref, nemb_ref, nacc_ref, nrel_ref, nracc_ref,
    total, half, in0, a1, in1, b1, in2, c1, in3, y1, a2, jn1, b2, jn2, c2, jn3, x2,
    e0, e1, hsum, nblk, ssem, rsem,
):
    d, m = lax.axis_index("dom"), lax.axis_index("edge")
    zl, c = m // 2, m % 2
    zh, x, y = d // 32, d // 8 % 4, d % 8
    z = zh * 2 + zl
    at = lambda x, y, z: ((z // 2) * 32 + x * 8 + y, (z % 2) * 2 + c)
    near, far = (d, zl * 2 + 1 - c), (d, (1 - zl) * 2 + c)
    xs = [at((x + s) % 4, y, z) for s in range(1, 4)]
    ys = [at(x, (y + s) % 8, z) for s in range(1, 8)]
    zs = [at(x, y, (z + s) % 8) for s in range(1, 8)]
    first = lambda s: at(x, (y + (1 - c) * s) % 8, (z + c * s) % 8)
    last = lambda s: at(x, (y + c * s) % 8, (z + (1 - c) * s) % 8)
    me1 = (1 - c) * y + c * z
    me3 = c * y + (1 - c) * z

    barrier = pltpu.get_barrier_semaphore()
    for device in [near] + xs + ys + zs:
        greet(barrier, device)
    pl.semaphore_wait(barrier, 18)

    sent = []

    def push(src, dst, phase, device):
        copy = remote(src, dst, ssem.at[phase], rsem.at[phase], device)
        copy.start()
        return copy

    other_half, own_half = pl.ds((1 - c) * 200, 200), pl.ds(c * 200, 200)
    push(grel_ref.at[other_half], in0, 0, near)
    for k in range(2):
        push(grad_ref.at[2 * k + 1 - c], e0.at[k], 1, near)

    drain(in0, rsem.at[0])
    a1[...] = grel_ref[pl.ds(c * 200, 100)] + in0[0:100]
    for s in range(1, 4):
        xx = (x + s) % 4
        push(a1.at[pl.ds(25 * xx, 25)], in1.at[x], 2, at(xx, y, z))
    a2[0:100] = grel_ref[pl.ds(c * 200 + 100, 100)] + in0[100:200]
    a2[100:104] = jnp.zeros((4, 8, 128), f32)
    for s in range(1, 8):
        push(a2.at[pl.ds(13 * ((me1 + s) % 8), 13)], jn1.at[me1], 3, first(s))

    drain(e0, rsem.at[1])
    for k in range(2):
        hsum[k] = grad_ref[2 * k + c] + e0[k]
    push(hsum.at[1 - zl], e1, 4, far)

    drain(in1.at[pl.ds(0, 3)], rsem.at[2])
    s1 = a1[pl.ds(25 * x, 25)]
    for s in range(1, 4):
        s1 = s1 + in1[(x + s) % 4]
    b1[0:25] = s1
    b1[25:32] = jnp.zeros((7, 8, 128), f32)
    for s in range(1, 8):
        yy = (y + s) % 8
        push(b1.at[pl.ds(4 * yy, 4)], in2.at[y], 5, at(x, yy, z))

    drain(jn1.at[pl.ds(0, 7)], rsem.at[3])
    s2 = a2[pl.ds(13 * me1, 13)]
    for s in range(1, 8):
        s2 = s2 + jn1[(me1 + s) % 8]
    b2[0:13] = s2
    b2[13:16] = jnp.zeros((3, 8, 128), f32)
    for s in range(1, 4):
        xx = (x + s) % 4
        push(b2.at[pl.ds(4 * xx, 4)], jn2.at[x], 6, at(xx, y, z))

    drain(in2.at[pl.ds(0, 7)], rsem.at[5])
    s1 = b1[pl.ds(4 * y, 4)]
    for s in range(1, 8):
        s1 = s1 + in2[(y + s) % 8]
    c1[...] = s1
    in3[z] = s1
    for s in range(1, 8):
        push(c1, in3.at[z], 7, zs[s - 1])

    drain(jn2.at[pl.ds(0, 3)], rsem.at[6])
    s2 = b2[pl.ds(4 * x, 4)]
    for s in range(1, 4):
        s2 = s2 + jn2[(x + s) % 4]
    c2[...] = s2
    jn3[me3] = s2
    for s in range(1, 8):
        push(c2, jn3.at[me3], 8, last(s))

    drain(e1, rsem.at[4])
    g = hsum[zl] + e1[...]
    mine = pl.ds(pl.multiple_of(m * 128, 128), 128)
    square = jnp.sum(jnp.sum(g * g, axis=0), axis=0, keepdims=True)
    new_acc = acc_ref[:, mine] + square * (1.0 / 400.0)
    step = learn_rate / jnp.sqrt(new_acc)
    nblk[m, 0:50] = emb_ref[:, mine].reshape(50, 8, 128) - g * step
    nblk[m, 50] = jnp.broadcast_to(new_acc, (8, 128))
    push(nblk.at[m], nblk.at[m], 9, far)
    push(nblk.at[m], nblk.at[m], 10, near)

    drain(in3.at[pl.ds(0, 7)], rsem.at[7])
    s1 = in3[0]
    for k in range(1, 8):
        s1 = s1 + in3[k]
    y1[pl.ds(4 * y, 4)] = s1
    for s in range(1, 8):
        push(y1.at[pl.ds(4 * y, 4)], y1.at[pl.ds(4 * y, 4)], 11, ys[s - 1])

    drain(jn3.at[pl.ds(0, 7)], rsem.at[8])
    s2 = jn3[0]
    for k in range(1, 8):
        s2 = s2 + jn3[k]
    x2[pl.ds(4 * x, 4)] = s2
    for s in range(1, 4):
        push(x2.at[pl.ds(4 * x, 4)], x2.at[pl.ds(4 * x, 4)], 12, xs[s - 1])

    far_m, near_m = (1 - zl) * 2 + c, zl * 2 + 1 - c
    drain(nblk.at[m], rsem.at[9])
    push(nblk.at[far_m], nblk.at[far_m], 13, near)

    drain(y1.at[pl.ds(0, 28)], rsem.at[11])
    base = c * 200
    for s in range(1, 4):
        push(y1.at[pl.ds(0, 25)], total.at[pl.ds(base + 25 * x, 25)], 14, xs[s - 1])
    total[pl.ds(base + 25 * x, 25)] = y1[0:25]

    drain(x2.at[pl.ds(0, 12)], rsem.at[12])
    for s in range(1, 8):
        push(x2.at[pl.ds(0, 13)], half.at[pl.ds(13 * me1, 13)], 15, first(s))
    half[pl.ds(13 * me1, 13)] = x2[0:13]

    drain(total.at[pl.ds(0, 75)], rsem.at[14])
    push(total.at[pl.ds(base, 100)], total.at[pl.ds(base, 100)], 16, near)

    drain(half.at[pl.ds(0, 91)], rsem.at[15])
    push(half.at[pl.ds(0, 100)], total.at[pl.ds(base + 100, 100)], 17, near)
    total[pl.ds(base + 100, 100)] = half[0:100]

    drain(nblk.at[m], rsem.at[10])
    drain(nblk.at[m], rsem.at[13])
    for k in range(4):
        nemb_ref[:, 128 * k : 128 * (k + 1)] = nblk[k, 0:50].reshape(400, 128)
        nacc_ref[:, 128 * k : 128 * (k + 1)] = nblk[k, 50, 0:1]

    drain(total.at[pl.ds(0, 100)], rsem.at[16])
    drain(total.at[pl.ds(0, 100)], rsem.at[17])
    for k in range(8):
        lanes = slice(128 * k, 128 * (k + 1))
        rows = [total[8 * i + k] for i in range(50)]
        square = rows[0] * rows[0]
        for v in rows[1:]:
            square = square + v * v
        new_racc = racc_ref[:, lanes] + jnp.sum(square, axis=0, keepdims=True) * (1.0 / 400.0)
        step = learn_rate / jnp.sqrt(new_racc)
        nracc_ref[:, lanes] = new_racc
        for i in range(50):
            nrel_ref[8 * i : 8 * i + 8, lanes] = rel_ref[8 * i : 8 * i + 8, lanes] - rows[i] * step

    drain(in0, ssem.at[0])
    drain(e0, ssem.at[1])
    drain(in1.at[pl.ds(0, 3)], ssem.at[2])
    drain(jn1.at[pl.ds(0, 7)], ssem.at[3])
    drain(e1, ssem.at[4])
    drain(in2.at[pl.ds(0, 7)], ssem.at[5])
    drain(jn2.at[pl.ds(0, 3)], ssem.at[6])
    drain(in3.at[pl.ds(0, 7)], ssem.at[7])
    drain(jn3.at[pl.ds(0, 7)], ssem.at[8])
    for p in (9, 10, 13):
        drain(nblk.at[0], ssem.at[p])
    drain(y1.at[pl.ds(0, 28)], ssem.at[11])
    drain(x2.at[pl.ds(0, 12)], ssem.at[12])
    drain(total.at[pl.ds(0, 75)], ssem.at[14])
    drain(half.at[pl.ds(0, 91)], ssem.at[15])
    drain(total.at[pl.ds(0, 100)], ssem.at[16])
    drain(total.at[pl.ds(0, 100)], ssem.at[17])


def reduce_update(grel, grad, emb, acc, relations, racc):
    t = lambda *lead: pltpu.VMEM((*lead, 8, 128), f32)
    shape = lambda *s: jax.ShapeDtypeStruct(s, f32)
    return pl.pallas_call(
        reduce_kernel,
        out_shape=(shape(400, 512), shape(1, 512), shape(400, 1024), shape(1, 1024)),
        in_specs=[VMEM] * 6,
        out_specs=(VMEM,) * 4,
        scratch_shapes=[
            t(400), t(104), t(200), t(100), t(4, 25), t(32), t(8, 4), t(4), t(8, 4), t(32),
            t(104), t(8, 13), t(16), t(4, 4), t(4), t(8, 4), t(16),
            t(2, 50), t(50), t(2, 50), t(4, 51),
            pltpu.SemaphoreType.DMA((18,)), pltpu.SemaphoreType.DMA((18,)),
        ],
        compiler_params=pltpu.CompilerParams(
            collective_id=2, has_side_effects=True, vmem_limit_bytes=56 * 2**20
        ),
        name="reduce_update",
    )(grel, grad, emb, acc, relations, racc)


def shards(embeddings, accum, relations, rel_accum, src_ids, rel_ids, dst_ids, neg_ids, bucket_len, partner):
    ids = jnp.concatenate([v.reshape(-1, 128) for v in (src_ids, rel_ids, dst_ids, neg_ids)], axis=0)
    position = lax.axis_index("edge") * 1024 + jnp.arange(1024, dtype=i32)
    live_src = jnp.where(position < bucket_len[0], src_ids[0], 512)
    own_ids = jnp.concatenate(
        [v.reshape(-1, 128) for v in (live_src, rel_ids, dst_ids, neg_ids)], axis=0
    )
    cols, pids = relay(ids, embeddings, bucket_len, partner)
    grel, grad = compute(embeddings, cols, relations, own_ids, pids)
    new_emb, new_acc, new_rel, new_racc = reduce_update(
        grel.reshape(400, 8, 128), grad, embeddings, accum.reshape(1, 512), relations, rel_accum.reshape(1, 1024)
    )
    return new_emb, new_acc.reshape(512), new_rel, new_racc.reshape(1024)


def solution(mesh):
    return jax.shard_map(
        shards,
        mesh=mesh,
        in_specs=(
            P(None, "dom"), P("dom"), P(), P(), P("dom", "edge"), P("dom", "edge"), P("dom", "edge"),
            P("dom", "edge", None), P("dom"), P(),
        ),
        out_specs=(P(None, "dom"), P("dom"), P(), P()),
        check_vma=False,
    )
```

```python
import jax
import jax.numpy as jnp
from jax import lax
from jax.experimental import pallas as pl
from jax.experimental.pallas import tpu as pltpu
from jax.sharding import PartitionSpec as P

MESH = pl.DeviceIdType.MESH
VMEM = pl.BlockSpec(memory_space=pltpu.VMEM)
SMEM = pl.BlockSpec(memory_space=pltpu.SMEM)
ANY = pl.BlockSpec(memory_space=pl.ANY)
f32, bf16, i32 = jnp.float32, jnp.bfloat16, jnp.int32
learn_rate = 0.1
HUBS = 32
ID_TILES = 5
SIZE = {"x": 4, "y": 8, "z": 8, "u": 8, "v": 8}
STREAMS = ((0, 4, "uxv"), (4, 2, "xyz"), (6, 2, "xzy"))


def remote(src, dst, send, recv, device):
    return pltpu.make_async_remote_copy(
        src_ref=src, dst_ref=dst, send_sem=send, recv_sem=recv, device_id=device, device_id_type=MESH
    )


def drain(ref, sem):
    pltpu.make_async_copy(ref, ref, sem).wait()


def levels(count, axes):
    n1 = -(-count // SIZE[axes[0]])
    return n1, -(-n1 // SIZE[axes[1]])


def stream_scratch(count, axes):
    n1, n2 = levels(count, axes)
    na, nb, nc = (SIZE[a] for a in axes)
    t = lambda *lead: pltpu.VMEM((*lead, 8, 128), f32)
    return [t(count), t(na * n1), t(na, n1), t(nb * n2), t(nb, n2), t(n2), t(nc, n2), t(nb * n2), t(na * n1)]


def onehots(out, ids, first, rows):
    for j in range(4):
        hit = lax.broadcasted_iota(i32, (rows, 128), 0) == ids[first + j : first + j + 1, :]
        out[:, 128 * j : 128 * (j + 1)] = jnp.where(hit, 1.0, 0.0).astype(bf16)


def split3(x):
    hi = x.astype(bf16)
    rest = x - hi.astype(f32)
    mid = rest.astype(bf16)
    lo = (rest - mid.astype(f32)).astype(bf16)
    return hi, mid, lo


def dot(a, b, ca=1, cb=0):
    return lax.dot_general(a, b, (((ca,), (cb,)), ((), ())), preferred_element_type=f32)


def add3(x):
    return x[0:400] + x[400:800] + x[800:1200]


def counts(ids, first):
    total = jnp.zeros((512, 128), f32)
    for j in range(8):
        hit = lax.broadcasted_iota(i32, (512, 128), 0) == ids[first + j : first + j + 1, :]
        total = total + jnp.where(hit, 1.0, 0.0)
    return dot(jnp.ones((8, 128), bf16), total.astype(bf16), 1, 1)[0:1]


def complex_product(a, b):
    return jnp.concatenate(
        [a[:200] * b[:200] - a[200:] * b[200:], a[:200] * b[200:] + a[200:] * b[:200]], axis=0
    )


def conj_product(a, b):
    return jnp.concatenate(
        [a[:200] * b[:200] + a[200:] * b[200:], a[200:] * b[:200] - a[:200] * b[200:]], axis=0
    )


def round_kernel(*refs):
    refs = list(refs)
    take = lambda n: [refs.pop(0) for _ in range(n)]
    src_in, rel_in, dst_in, neg_in, emb_in, acc_in, relations_in, len_ref, partner_ref = take(9)
    total, nblk = take(2)
    src_v, rel_v, dst_v, neg_v, emb, acc, relations, in_sem = take(8)
    pay, hub, stage, got, cols, send1, recv1, gsend, grecv, send2, recv2, asend, arecv = take(13)
    ids, pids, own_b, other_b, rel3, oh_src, oh_dst, oh_rel, p_src, p_dst, p_rel = take(11)
    h_s, r_s, q_s, dq_s, pr_s, dr3, parts, gt, dn, grel, grad = take(11)
    e0, e1, hsum, esend, erecv, ssem, rsem = take(7)
    streams = [(axes, 25 * n, 25 * lane, take(9)) for lane, n, axes in STREAMS]

    d, m = lax.axis_index("dom"), lax.axis_index("edge")
    zl, c = m // 2, m % 2
    zh, x, y = d // 32, d // 8 % 4, d % 8
    z = zh * 2 + zl
    at = lambda x, y, z: ((z // 2) * 32 + x * 8 + y, (z % 2) * 2 + c)
    far_m, near_m = (1 - zl) * 2 + c, zl * 2 + 1 - c
    far, near = (d, far_m), (d, near_m)
    spoke_m = (d + 3) % 4
    mine = pl.ds(pl.multiple_of(m * 128, 128), 128)
    place = {"x": x, "y": y, "z": z, "u": (1 - c) * y + c * z, "v": c * y + (1 - c) * z}
    peer = {
        "x": lambda s: at((x + s) % 4, y, z),
        "y": lambda s: at(x, (y + s) % 8, z),
        "z": lambda s: at(x, y, (z + s) % 8),
        "u": lambda s: at(x, (y + (1 - c) * s) % 8, (z + c * s) % 8),
        "v": lambda s: at(x, (y + c * s) % 8, (z + (1 - c) * s) % 8),
    }

    barrier = pltpu.get_barrier_semaphore()
    greet = lambda device: pl.semaphore_signal(barrier, inc=1, device_id=device, device_id_type=MESH)
    inputs = [
        pltpu.make_async_copy(a, b, in_sem.at[i])
        for i, (a, b) in enumerate(
            [(src_in, src_v), (rel_in, rel_v), (dst_in, dst_v), (neg_in, neg_v), (emb_in, emb), (acc_in, acc),
             (relations_in, relations)]
        )
    ]
    for copy in inputs:
        copy.start()

    def hello(j, _):
        greet((4 * j + m, spoke_m))
        return 0

    lax.fori_loop(0, HUBS, hello, 0)
    greet(near)
    for axis in "xyz":
        for s in range(1, SIZE[axis]):
            greet(peer[axis](s))

    for copy in inputs[:5]:
        copy.wait()
    pay[0:25] = emb[:, mine].astype(bf16).reshape(25, 16, 128)
    slot = m * 1024 + lax.broadcasted_iota(i32, (8, 128), 0) * 128 + lax.broadcasted_iota(i32, (8, 128), 1)
    rows = [src_v, rel_v, dst_v, neg_v.at[0, 0:1], neg_v.at[0, 1:2]]
    for a, row in enumerate(rows):
        for j in range(8):
            ids[8 * a + j : 8 * a + j + 1, :] = row[0:1, 128 * j : 128 * (j + 1)]
        v = ids[8 * a : 8 * a + 8, :]
        if a == 0:
            v = jnp.where(slot < len_ref[0], v, 512)
            ids[0:8, :] = v
        pay[25 + a] = jnp.concatenate([(v >> 5).astype(f32), (v & 31).astype(f32)], axis=0).astype(bf16)
    pay[30:32] = jnp.zeros((2, 16, 128), bf16)
    pl.semaphore_wait(barrier, HUBS + 18)

    def leg1(i, _):
        remote(pay.at[i], hub.at[d % 4, d // 4], send1, recv1, (4 * i + (m + 1) % 4, d % 4)).start()
        return 0

    lax.fori_loop(0, HUBS, leg1, 0)

    lanes = [slice(0, 512), slice(512, 1024)]

    def gather_rel(hot, ids, k, out):
        onehots(hot, ids, 8 + 4 * k, 1024)
        out[:, lanes[k]] = add3(dot(rel3[...], hot[...]))

    def own_start(k):
        onehots(oh_src.at[:, lanes[k]], ids, 4 * k, 512)
        h = dot(own_b[...], oh_src[:, lanes[k]])
        h_s[:, lanes[k]] = h
        q_s[:, lanes[k]] = complex_product(h, r_s[:, lanes[k]])
        onehots(oh_dst.at[:, lanes[k]], ids, 16 + 4 * k, 512)

    own_b[...] = emb[...].astype(bf16)
    inputs[6].wait()
    rel3[0:400], rel3[400:800], rel3[800:1200] = split3(relations[...])
    gather_rel(oh_rel.at[:, lanes[0]], ids, 0, r_s)

    drain(hub.at[m], recv1)
    g_far = remote(hub.at[m], hub.at[m], gsend.at[0], grecv.at[0], far)
    g_near = remote(hub.at[m], hub.at[m], gsend.at[1], grecv.at[1], near)
    g_far.start()
    g_near.start()
    gather_rel(oh_rel.at[:, lanes[1]], ids, 1, r_s)
    g_far.wait_recv()
    g_fwd = remote(hub.at[far_m], hub.at[far_m], gsend.at[2], grecv.at[2], near)
    g_fwd.start()
    g_near.wait_recv()
    g_fwd.wait_recv()

    def leg2(j, _):
        t = 4 * j + m
        p = partner_ref[t]
        stage[j] = hub[p % 4, p // 4]
        remote(stage.at[j], got.at[d // 4], send2, recv2, (t, spoke_m)).start()
        return 0

    lax.fori_loop(0, HUBS, leg2, 0)
    own_start(0)
    own_start(1)
    count = [counts(ids, 24 + 8 * k) for k in range(2)]
    drain(got, recv2)

    block = got.at[pl.ds(0, 25)]
    a_far = remote(block, cols.at[m], asend.at[0], arecv.at[0], far)
    a_near = remote(block, cols.at[m], asend.at[1], arecv.at[1], near)
    a_far.start()
    a_near.start()
    cols[m] = got[0:25]
    for a in range(ID_TILES):
        v = got[25 + a].astype(f32)
        pids[8 * a : 8 * a + 8, :] = (v[:8] * 32.0 + v[8:]).astype(i32)
    gather_rel(p_rel, pids, 0, pr_s)
    a_far.wait_recv()
    a_fwd = remote(cols.at[far_m], cols.at[far_m], asend.at[2], arecv.at[2], near)
    a_fwd.start()
    gather_rel(p_rel, pids, 1, pr_s)
    a_near.wait_recv()
    a_fwd.wait_recv()
    for k in range(4):
        other_b[:, 128 * k : 128 * (k + 1)] = cols[k].reshape(400, 128)

    for k in range(2):
        q = q_s[:, lanes[k]]
        t = dot(other_b[...], oh_dst[:, lanes[k]])
        g_pos = -jax.nn.sigmoid(-jnp.sum(q * t, axis=0, keepdims=True))
        negs = dot(other_b[...], q.astype(bf16), 0, 0)
        gt[...] = (jax.nn.sigmoid(negs) * 0.03125).astype(bf16)
        weighted = other_b[...].astype(f32) * count[k]
        w_hi = weighted.astype(bf16)
        w_lo = (weighted - w_hi.astype(f32)).astype(bf16)
        dq = t * g_pos + dot(w_hi, gt[...]) + dot(w_lo, gt[...])
        dq_s[:, lanes[k]] = dq
        for i, v in enumerate(split3(conj_product(dq, h_s[:, lanes[k]]))):
            dr3[400 * i : 400 * (i + 1), lanes[k]] = v

    def rel_scatter(n):
        g = add3(dot(dr3[...], oh_rel[256 * n : 256 * (n + 1), :], 1, 1))
        for j in range(2):
            for half in range(2):
                grel[half, pl.ds(25 * (2 * n + j), 25)] = g[
                    200 * half : 200 * (half + 1), 128 * j : 128 * (j + 1)
                ].reshape(25, 8, 128)

    def step(i, level):
        axes, T, base, (in0, a, in1, b, in2, last, in3, gb, ga) = streams[i]
        n1, n2 = levels(T, axes)
        (A, B, C), (na, nb, nc) = axes, [SIZE[k] for k in axes]
        ma, mb, mc = place[A], place[B], place[C]
        zeros = lambda n: jnp.zeros((n, 8, 128), f32)

        def push(src, dst, device):
            remote(src, dst, ssem.at[i, level], rsem.at[i, level], device).start()

        if level == 0:
            push(grel.at[1 - c, pl.ds(base, T)], in0, near)
        elif level == 1:
            drain(in0, rsem.at[i, 0])
            a[0:T] = grel[c, pl.ds(base, T)] + in0[...]
            if na * n1 > T:
                a[T : na * n1] = zeros(na * n1 - T)
            for s in range(1, na):
                push(a.at[pl.ds(n1 * ((ma + s) % na), n1)], in1.at[ma], peer[A](s))
        elif level == 2:
            drain(in1.at[pl.ds(0, na - 1)], rsem.at[i, 1])
            v = a[pl.ds(n1 * ma, n1)]
            for s in range(1, na):
                v = v + in1[(ma + s) % na]
            b[0:n1] = v
            if nb * n2 > n1:
                b[n1 : nb * n2] = zeros(nb * n2 - n1)
            for s in range(1, nb):
                push(b.at[pl.ds(n2 * ((mb + s) % nb), n2)], in2.at[mb], peer[B](s))
        elif level == 3:
            drain(in2.at[pl.ds(0, nb - 1)], rsem.at[i, 2])
            v = b[pl.ds(n2 * mb, n2)]
            for s in range(1, nb):
                v = v + in2[(mb + s) % nb]
            last[...] = v
            in3[mc] = v
            for s in range(1, nc):
                push(last, in3.at[mc], peer[C](s))
        elif level == 4:
            drain(in3.at[pl.ds(0, nc - 1)], rsem.at[i, 3])
            v = in3[0]
            for s in range(1, nc):
                v = v + in3[s]
            spot = pl.ds(n2 * mb, n2)
            gb[spot] = v
            for s in range(1, nb):
                push(gb.at[spot], gb.at[spot], peer[B](s))
        elif level == 5:
            drain(gb.at[pl.ds(0, (nb - 1) * n2)], rsem.at[i, 4])
            spot = pl.ds(n1 * ma, n1)
            for s in range(1, na):
                push(gb.at[pl.ds(0, n1)], ga.at[spot], peer[A](s))
            ga[spot] = gb[0:n1]
        elif level == 6:
            drain(ga.at[pl.ds(0, (na - 1) * n1)], rsem.at[i, 5])
            push(ga.at[pl.ds(0, T)], total.at[c, pl.ds(base, T)], near)
            total[c, pl.ds(base, T)] = ga[0:T]
        else:
            drain(in0, rsem.at[i, 6])
            drain(in0, ssem.at[i, 0])
            drain(in1.at[pl.ds(0, na - 1)], ssem.at[i, 1])
            drain(in2.at[pl.ds(0, nb - 1)], ssem.at[i, 2])
            drain(in3.at[pl.ds(0, nc - 1)], ssem.at[i, 3])
            drain(gb.at[pl.ds(0, (nb - 1) * n2)], ssem.at[i, 4])
            drain(ga.at[pl.ds(0, (na - 1) * n1)], ssem.at[i, 5])
            drain(in0, ssem.at[i, 6])

    held = {}

    def partner_a(k):
        onehots(p_src, pids, 4 * k, 512)
        onehots(p_dst.at[:, lanes[k]], pids, 16 + 4 * k, 512)
        h = dot(other_b[...], p_src[...])
        t = dot(own_b[...], p_dst[:, lanes[k]])
        q = complex_product(h, pr_s[:, lanes[k]])
        q_s[:, lanes[k]] = q
        g_pos = -jax.nn.sigmoid(-jnp.sum(q * t, axis=0, keepdims=True))
        for i, v in enumerate(split3(q * g_pos)):
            parts[400 * i : 400 * (i + 1), lanes[k]] = v

    def partner_b(k):
        q_b = q_s[:, lanes[k]].astype(bf16)
        gt[...] = (jax.nn.sigmoid(dot(own_b[...], q_b, 0, 0)) * 0.03125).astype(bf16)
        v = dot(q_b, gt[...], 1, 1) * counts(pids, 24 + 8 * k)
        dn[...] = v if k == 0 else dn[...] + v

    def dh(k):
        for i, v in enumerate(split3(conj_product(dq_s[:, lanes[k]], r_s[:, lanes[k]]))):
            dr3[400 * i : 400 * (i + 1), lanes[k]] = v

    def ent_scatter(n):
        rows = slice(256 * n, 256 * (n + 1))
        g = add3(dot(dr3[...], oh_src[rows, :], 1, 1) + dot(parts[...], p_dst[rows, :], 1, 1)) + dn[:, rows]
        for j in range(2):
            grad[2 * n + j] = g[:, 128 * j : 128 * (j + 1)].reshape(50, 8, 128)

    def ent(level):
        def push(src, dst, device):
            remote(src, dst, esend.at[level], erecv.at[level], device).start()

        if level == 0:
            for k in range(2):
                push(grad.at[2 * k + 1 - c], e0.at[k], near)
        elif level == 1:
            drain(e0, erecv.at[0])
            for k in range(2):
                hsum[k] = grad[2 * k + c] + e0[k]
            push(hsum.at[1 - zl], e1, far)
        elif level == 2:
            drain(e1, erecv.at[1])
            g = hsum[zl] + e1[...]
            square = jnp.sum(jnp.sum(g * g, axis=0), axis=0, keepdims=True)
            new_acc = acc[:, mine] + square * (1.0 / 400.0)
            nblk[m, 0:50] = emb[:, mine].reshape(50, 8, 128) - g * (learn_rate / jnp.sqrt(new_acc))
            nblk[m, 50] = jnp.broadcast_to(new_acc, (8, 128))
            push(nblk.at[m], nblk.at[m], far)
        elif level == 3:
            push(nblk.at[m], nblk.at[m], near)
        elif level == 4:
            drain(nblk.at[m], erecv.at[2])
            push(nblk.at[far_m], nblk.at[far_m], near)
        else:
            drain(nblk.at[m], erecv.at[3])
            drain(nblk.at[m], erecv.at[4])
            drain(e0, esend.at[0])
            drain(e1, esend.at[1])
            for k in range(2, 5):
                drain(nblk.at[m], esend.at[k])

    rel_scatter(0)
    rel_scatter(1)
    step(0, 0)
    rel_scatter(2)
    step(1, 0)
    step(0, 1)
    rel_scatter(3)
    step(2, 0)
    step(1, 1)
    step(2, 1)
    inputs[5].wait()
    dh(0)
    dh(1)
    partner_a(0)
    step(1, 2)
    partner_b(0)
    step(2, 2)
    step(0, 2)
    partner_a(1)
    step(1, 3)
    step(0, 3)
    step(2, 3)
    partner_b(1)
    ent_scatter(0)
    step(1, 4)
    step(0, 4)
    ent_scatter(1)
    ent(0)
    step(2, 4)
    step(1, 5)
    step(0, 5)
    ent(1)
    step(2, 5)
    step(1, 6)
    step(0, 6)
    ent(2)
    ent(3)
    step(2, 6)
    ent(4)
    ent(5)
    for i in range(3):
        step(i, 7)

    for copy in (g_far, g_near, g_fwd, a_far, a_near, a_fwd):
        copy.wait_send()
    drain(pay, send1)
    drain(stage, send2)


def bucket_round(*args):
    tile = lambda *lead: pltpu.VMEM((*lead, 16, 128), bf16)
    t = lambda *lead: pltpu.VMEM((*lead, 8, 128), f32)
    V = pltpu.VMEM
    dma = pltpu.SemaphoreType.DMA
    scratch = [
        V((1, 1024), i32), V((1, 1024), i32), V((1, 1024), i32), V((1, 2, 1024), i32), V((400, 512), f32),
        V((1, 512), f32), V((400, 1024), f32), dma((7,)),
        tile(32), tile(4, 32), tile(32), tile(32), tile(4, 25),
        dma, dma, dma((3,)), dma((3,)), dma, dma, dma((3,)), dma((3,)),
        V((40, 128), i32), V((40, 128), i32), V((400, 512), bf16), V((400, 512), bf16), V((1200, 1024), bf16),
        V((512, 1024), bf16), V((512, 1024), bf16), V((1024, 1024), bf16),
        V((512, 512), bf16), V((512, 1024), bf16), V((1024, 512), bf16),
        V((400, 1024), f32), V((400, 1024), f32), V((400, 1024), f32), V((400, 1024), f32), V((400, 1024), f32),
        V((1200, 1024), bf16), V((1200, 1024), bf16), V((512, 512), bf16), V((400, 512), f32),
        t(2, 200), t(4, 50),
        t(2, 50), t(50), t(2, 50), dma((5,)), dma((5,)), dma((3, 7)), dma((3, 7)),
    ]
    for _, n, axes in STREAMS:
        scratch += stream_scratch(25 * n, axes)
    return pl.pallas_call(
        round_kernel,
        out_shape=(jax.ShapeDtypeStruct((2, 200, 8, 128), f32), jax.ShapeDtypeStruct((4, 51, 8, 128), f32)),
        in_specs=[ANY] * 7 + [SMEM] * 2,
        out_specs=(VMEM, VMEM),
        scratch_shapes=scratch,
        compiler_params=pltpu.CompilerParams(
            collective_id=1, has_side_effects=True, vmem_limit_bytes=56 * 2**20
        ),
        name="bucket_round",
    )(*args)


def update_kernel(total, nblk, rel_ref, racc_ref, nemb_ref, nacc_ref, nrel_ref, nracc_ref):
    for k in range(8):
        lanes = slice(128 * k, 128 * (k + 1))
        square = jnp.zeros((8, 128), f32)
        for half in range(2):
            for i in range(25):
                v = total[half, 25 * k + i]
                square = square + v * v
        new_racc = racc_ref[:, lanes] + jnp.sum(square, axis=0, keepdims=True) * (1.0 / 400.0)
        rate = learn_rate / jnp.sqrt(new_racc)
        nracc_ref[:, lanes] = new_racc
        for half in range(2):
            rows = slice(200 * half, 200 * (half + 1))
            g = total[half, 25 * k : 25 * (k + 1)].reshape(200, 128)
            nrel_ref[rows, lanes] = rel_ref[rows, lanes] - g * rate
    for k in range(4):
        lanes = slice(128 * k, 128 * (k + 1))
        nemb_ref[:, lanes] = nblk[k, 0:50].reshape(400, 128)
        nacc_ref[:, lanes] = nblk[k, 50, 0:1]


def update(total, nblk, relations, racc):
    shape = lambda *s: jax.ShapeDtypeStruct(s, f32)
    return pl.pallas_call(
        update_kernel,
        out_shape=(shape(400, 512), shape(1, 512), shape(400, 1024), shape(1, 1024)),
        in_specs=[VMEM] * 4,
        out_specs=(VMEM,) * 4,
        compiler_params=pltpu.CompilerParams(vmem_limit_bytes=32 * 2**20),
        name="update",
    )(total, nblk, relations, racc)


def shards(embeddings, accum, relations, rel_accum, src_ids, rel_ids, dst_ids, neg_ids, bucket_len, partner):
    total, nblk = bucket_round(
        src_ids, rel_ids, dst_ids, neg_ids, embeddings, accum.reshape(1, 512), relations, bucket_len, partner
    )
    new_emb, new_acc, new_rel, new_racc = update(total, nblk, relations, rel_accum.reshape(1, 1024))
    return new_emb, new_acc.reshape(512), new_rel, new_racc.reshape(1024)


def solution(mesh):
    return jax.shard_map(
        shards,
        mesh=mesh,
        in_specs=(
            P(None, "dom"), P("dom"), P(), P(), P("dom", "edge"), P("dom", "edge"), P("dom", "edge"),
            P("dom", "edge", None), P("dom"), P(),
        ),
        out_specs=(P(None, "dom"), P("dom"), P(), P()),
        check_vma=False,
    )
```

```python
import jax
import jax.numpy as jnp
from jax import lax
from jax.experimental import pallas as pl
from jax.experimental.pallas import tpu as pltpu
from jax.sharding import PartitionSpec as P

MESH = pl.DeviceIdType.MESH
VMEM = pl.BlockSpec(memory_space=pltpu.VMEM)
SMEM = pl.BlockSpec(memory_space=pltpu.SMEM)
ANY = pl.BlockSpec(memory_space=pl.ANY)
f32, bf16, i32 = jnp.float32, jnp.bfloat16, jnp.int32
learn_rate = 0.1
HUBS = 32
ID_TILES = 5
SIZE = {"x": 4, "y": 8, "z": 8, "u": 8, "v": 8}
STREAMS = ((0, 2, "uxv"), (2, 2, "vxu"), (4, 2, "xyz"), (6, 2, "xzy"))


def remote(src, dst, send, recv, device):
    return pltpu.make_async_remote_copy(
        src_ref=src, dst_ref=dst, send_sem=send, recv_sem=recv, device_id=device, device_id_type=MESH
    )


def drain(ref, sem):
    pltpu.make_async_copy(ref, ref, sem).wait()


def levels(count, axes):
    n1 = -(-count // SIZE[axes[0]])
    return n1, -(-n1 // SIZE[axes[1]])


def stream_scratch(count, axes):
    n1, n2 = levels(count, axes)
    na, nb, nc = (SIZE[a] for a in axes)
    t = lambda *lead: pltpu.VMEM((*lead, 8, 128), f32)
    return [t(count), t(na * n1), t(na, n1), t(nb * n2), t(nb, n2), t(n2), t(nc, n2), t(nb * n2), t(na * n1)]


def onehots(out, ids, first, rows):
    for j in range(4):
        hit = lax.broadcasted_iota(i32, (rows, 128), 0) == ids[first + j : first + j + 1, :]
        out[:, 128 * j : 128 * (j + 1)] = jnp.where(hit, 1.0, 0.0).astype(bf16)


def split3(x):
    hi = x.astype(bf16)
    rest = x - hi.astype(f32)
    mid = rest.astype(bf16)
    lo = (rest - mid.astype(f32)).astype(bf16)
    return hi, mid, lo


def dot(a, b, ca=1, cb=0):
    return lax.dot_general(a, b, (((ca,), (cb,)), ((), ())), preferred_element_type=f32)


def add3(x):
    return x[0:400] + x[400:800] + x[800:1200]


def counts(ids, first):
    total = jnp.zeros((512, 128), f32)
    for j in range(8):
        hit = lax.broadcasted_iota(i32, (512, 128), 0) == ids[first + j : first + j + 1, :]
        total = total + jnp.where(hit, 1.0, 0.0)
    return dot(jnp.ones((8, 128), bf16), total.astype(bf16), 1, 1)[0:1]


def complex_product(a, b):
    return jnp.concatenate(
        [a[:200] * b[:200] - a[200:] * b[200:], a[:200] * b[200:] + a[200:] * b[:200]], axis=0
    )


def conj_product(a, b):
    return jnp.concatenate(
        [a[:200] * b[:200] + a[200:] * b[200:], a[200:] * b[:200] - a[:200] * b[200:]], axis=0
    )


def round_kernel(*refs):
    refs = list(refs)
    take = lambda n: [refs.pop(0) for _ in range(n)]
    src_in, rel_in, dst_in, neg_in, emb_in, acc_in, relations_in, len_ref, partner_ref = take(9)
    total, nemb_out, nacc_out = take(3)
    src_v, rel_v, dst_v, neg_v, emb, acc, relations, in_sem = take(8)
    pay, hub, stage, got, cols, nblk, send1, recv1, gsend, grecv, send2, recv2, asend, arecv = take(14)
    ids, pids, own_b, other_b, rel3, oh_src, oh_dst, oh_rel, p_src, p_dst, p_rel = take(11)
    h_s, r_s, q_s, qb_s, t_s, dq_s, pr_s, cnt, dr3, parts, gt, dn, grel, grad = take(14)
    e0, e1, hsum, esend, erecv, ssem, rsem, osem = take(8)
    streams = [(axes, 25 * n, 25 * lane, take(9)) for lane, n, axes in STREAMS]

    d, m = lax.axis_index("dom"), lax.axis_index("edge")
    zl, c = m // 2, m % 2
    zh, x, y = d // 32, d // 8 % 4, d % 8
    z = zh * 2 + zl
    at = lambda x, y, z: ((z // 2) * 32 + x * 8 + y, (z % 2) * 2 + c)
    far_m, near_m = (1 - zl) * 2 + c, zl * 2 + 1 - c
    far, near = (d, far_m), (d, near_m)
    spoke_m = (d + 3) % 4
    is_hub = (d // 8 + spoke_m) % 2 == zl
    order = lambda k: 2 + (k + 1) // 2 * (1 - 2 * (k % 2))

    def spoke(j):
        near_y, near_x, near_z = order(j // 4 % 4), order(j % 4), order(j // 16)
        return (zh + near_z) % 4 * 32 + (x + near_x) % 4 * 8 + (y // 2 + near_y) % 4 * 2 + c

    mine = pl.ds(pl.multiple_of(m * 128, 128), 128)
    place = {"x": x, "y": y, "z": z, "u": (1 - c) * y + c * z, "v": c * y + (1 - c) * z}
    peer = {
        "x": lambda s: at((x + s) % 4, y, z),
        "y": lambda s: at(x, (y + s) % 8, z),
        "z": lambda s: at(x, y, (z + s) % 8),
        "u": lambda s: at(x, (y + (1 - c) * s) % 8, (z + c * s) % 8),
        "v": lambda s: at(x, (y + c * s) % 8, (z + (1 - c) * s) % 8),
    }

    barrier = pltpu.get_barrier_semaphore()
    greet = lambda device: pl.semaphore_signal(barrier, inc=1, device_id=device, device_id_type=MESH)
    inputs = [
        pltpu.make_async_copy(a, b, in_sem.at[i])
        for i, (a, b) in enumerate(
            [(src_in, src_v), (rel_in, rel_v), (dst_in, dst_v), (neg_in, neg_v), (emb_in, emb), (acc_in, acc),
             (relations_in, relations)]
        )
    ]
    for copy in inputs:
        copy.start()

    def hello(j, _):
        greet((spoke(j), spoke_m))
        return 0

    @pl.when(is_hub)
    def _():
        lax.fori_loop(0, 64, hello, 0)

    greet(near)
    for axis in "xyz":
        for s in range(1, SIZE[axis]):
            greet(peer[axis](s))

    for copy in inputs[:5]:
        copy.wait()
    pay[0:25] = emb[:, mine].astype(bf16).reshape(25, 16, 128)
    slot = m * 1024 + lax.broadcasted_iota(i32, (8, 128), 0) * 128 + lax.broadcasted_iota(i32, (8, 128), 1)
    rows = [src_v, rel_v, dst_v, neg_v.at[0, 0:1], neg_v.at[0, 1:2]]
    for a, row in enumerate(rows):
        for j in range(8):
            ids[8 * a + j : 8 * a + j + 1, :] = row[0:1, 128 * j : 128 * (j + 1)]
        v = ids[8 * a : 8 * a + 8, :]
        if a == 0:
            v = jnp.where(slot < len_ref[0], v, 512)
            ids[0:8, :] = v
        pay[25 + a] = jnp.concatenate([(v >> 5).astype(f32), (v & 31).astype(f32)], axis=0).astype(bf16)
    pay[30:32] = jnp.zeros((2, 16, 128), bf16)
    pl.semaphore_wait(barrier, HUBS + 18)

    def leg1(i, _):
        i = (zh + order(i // 8)) % 4 * 8 + (x + order(i % 4)) % 4 * 2 + (y // 4 + 1 + i // 4) % 2
        device = (4 * i + (m + 1) % 4, (i // 2 + m) % 2 * 2 + d % 2)
        remote(pay.at[i], hub.at[d % 2, d // 2], send1, recv1, device).start()
        return 0

    lax.fori_loop(0, HUBS, leg1, 0)

    lanes = [slice(0, 512), slice(512, 1024)]

    def gather_rel(hot, ids, k, out):
        onehots(hot, ids, 8 + 4 * k, 1024)
        out[:, lanes[k]] = add3(dot(rel3[...], hot[...]))

    def own_start(k):
        onehots(oh_src.at[:, lanes[k]], ids, 4 * k, 512)
        h = dot(own_b[...], oh_src[:, lanes[k]])
        h_s[:, lanes[k]] = h
        q = complex_product(h, r_s[:, lanes[k]])
        q_s[:, lanes[k]] = q
        qb_s[:, lanes[k]] = q.astype(bf16)
        onehots(oh_dst.at[:, lanes[k]], ids, 16 + 4 * k, 512)

    own_b[...] = emb[...].astype(bf16)
    inputs[6].wait()
    rel3[0:400], rel3[400:800], rel3[800:1200] = split3(relations[...])
    gather_rel(oh_rel.at[:, lanes[0]], ids, 0, r_s)

    def leg2(j, _):
        t = spoke(j)
        p = partner_ref[t]
        stage[j] = hub[p % 2, p // 2]
        remote(stage.at[j], got.at[d // 4], send2, recv2, (t, spoke_m)).start()
        return 0

    @pl.when(is_hub)
    def _():
        drain(hub.at[c], recv1)
        share = remote(hub.at[c], hub.at[c], gsend, grecv, near)
        share.start()
        share.wait()
        lax.fori_loop(0, 64, leg2, 0)

    gather_rel(oh_rel.at[:, lanes[1]], ids, 1, r_s)
    own_start(0)
    own_start(1)
    for k in range(2):
        cnt[k : k + 1, :] = counts(ids, 24 + 8 * k)
    drain(got, recv2)

    block = got.at[pl.ds(0, 25)]
    a_far = remote(block, cols.at[m], asend.at[0], arecv.at[0], far)
    a_near = remote(block, cols.at[m], asend.at[1], arecv.at[1], near)
    a_far.start()
    a_near.start()

    def place_cols(k, value):
        other_b[:, pl.ds(pl.multiple_of(k * 128, 128), 128)] = value.reshape(400, 128)

    def own_part(k, pair):
        ents = pl.ds(pl.multiple_of(pair * 256, 256), 256)
        part = other_b[:, ents]
        t = dot(part, oh_dst[ents, lanes[k]])
        negs = dot(part, qb_s[:, lanes[k]], 0, 0)
        g = (jax.nn.sigmoid(negs) * 0.03125).astype(bf16)
        weighted = part.astype(f32) * cnt[k : k + 1, ents]
        w_hi = weighted.astype(bf16)
        w_lo = (weighted - w_hi.astype(f32)).astype(bf16)
        return t, dot(w_hi, g) + dot(w_lo, g)

    place_cols(m, got[0:25])
    cols[m] = got[0:25]
    for a in range(ID_TILES):
        v = got[25 + a].astype(f32)
        pids[8 * a : 8 * a + 8, :] = (v[:8] * 32.0 + v[8:]).astype(i32)
    gather_rel(p_rel, pids, 0, pr_s)
    a_near.wait_recv()
    place_cols(near_m, cols[near_m])
    for k in range(2):
        t_s[:, lanes[k]], dq_s[:, lanes[k]] = own_part(k, zl)
    a_far.wait_recv()
    a_fwd = remote(cols.at[far_m], cols.at[far_m], asend.at[2], arecv.at[2], near)
    a_fwd.start()
    place_cols(far_m, cols[far_m])
    gather_rel(p_rel, pids, 1, pr_s)
    a_fwd.wait_recv()
    place_cols(3 - m, cols[3 - m])

    for k in range(2):
        t, back = own_part(k, 1 - zl)
        t = t + t_s[:, lanes[k]]
        g_pos = -jax.nn.sigmoid(-jnp.sum(q_s[:, lanes[k]] * t, axis=0, keepdims=True))
        dq = t * g_pos + (dq_s[:, lanes[k]] + back)
        dq_s[:, lanes[k]] = dq
        for i, v in enumerate(split3(conj_product(dq, h_s[:, lanes[k]]))):
            dr3[400 * i : 400 * (i + 1), lanes[k]] = v

    def rel_scatter(n):
        g = add3(dot(dr3[...], oh_rel[256 * n : 256 * (n + 1), :], 1, 1))
        for j in range(2):
            for half in range(2):
                grel[half, pl.ds(25 * (2 * n + j), 25)] = g[
                    200 * half : 200 * (half + 1), 128 * j : 128 * (j + 1)
                ].reshape(25, 8, 128)

    def step(i, level):
        axes, T, base, (in0, a, in1, b, in2, last, in3, gb, ga) = streams[i]
        n1, n2 = levels(T, axes)
        (A, B, C), (na, nb, nc) = axes, [SIZE[k] for k in axes]
        ma, mb, mc = place[A], place[B], place[C]
        zeros = lambda n: jnp.zeros((n, 8, 128), f32)

        def push(src, dst, device):
            remote(src, dst, ssem.at[i, level], rsem.at[i, level], device).start()

        if level == 0:
            push(grel.at[1 - c, pl.ds(base, T)], in0, near)
        elif level == 1:
            drain(in0, rsem.at[i, 0])
            a[0:T] = grel[c, pl.ds(base, T)] + in0[...]
            if na * n1 > T:
                a[T : na * n1] = zeros(na * n1 - T)
            for s in range(1, na):
                push(a.at[pl.ds(n1 * ((ma + s) % na), n1)], in1.at[ma], peer[A](s))
        elif level == 2:
            drain(in1.at[pl.ds(0, na - 1)], rsem.at[i, 1])
            v = a[pl.ds(n1 * ma, n1)]
            for s in range(1, na):
                v = v + in1[(ma + s) % na]
            b[0:n1] = v
            if nb * n2 > n1:
                b[n1 : nb * n2] = zeros(nb * n2 - n1)
            for s in range(1, nb):
                push(b.at[pl.ds(n2 * ((mb + s) % nb), n2)], in2.at[mb], peer[B](s))
        elif level == 3:
            drain(in2.at[pl.ds(0, nb - 1)], rsem.at[i, 2])
            v = b[pl.ds(n2 * mb, n2)]
            for s in range(1, nb):
                v = v + in2[(mb + s) % nb]
            last[...] = v
            in3[mc] = v
            for s in range(1, nc):
                push(last, in3.at[mc], peer[C](s))
        elif level == 4:
            drain(in3.at[pl.ds(0, nc - 1)], rsem.at[i, 3])
            v = in3[0]
            for s in range(1, nc):
                v = v + in3[s]
            spot = pl.ds(n2 * mb, n2)
            gb[spot] = v
            for s in range(1, nb):
                push(gb.at[spot], gb.at[spot], peer[B](s))
        elif level == 5:
            drain(gb.at[pl.ds(0, (nb - 1) * n2)], rsem.at[i, 4])
            spot = pl.ds(n1 * ma, n1)
            for s in range(1, na):
                push(gb.at[pl.ds(0, n1)], ga.at[spot], peer[A](s))
            ga[spot] = gb[0:n1]
        elif level == 6:
            drain(ga.at[pl.ds(0, (na - 1) * n1)], rsem.at[i, 5])
            push(ga.at[pl.ds(0, T)], total.at[c, pl.ds(base, T)], near)
            pltpu.make_async_copy(ga.at[pl.ds(0, T)], total.at[c, pl.ds(base, T)], osem.at[i]).start()
        else:
            drain(in0, osem.at[i])
            drain(in0, rsem.at[i, 6])
            drain(in0, ssem.at[i, 0])
            drain(in1.at[pl.ds(0, na - 1)], ssem.at[i, 1])
            drain(in2.at[pl.ds(0, nb - 1)], ssem.at[i, 2])
            drain(in3.at[pl.ds(0, nc - 1)], ssem.at[i, 3])
            drain(gb.at[pl.ds(0, (nb - 1) * n2)], ssem.at[i, 4])
            drain(ga.at[pl.ds(0, (na - 1) * n1)], ssem.at[i, 5])
            drain(in0, ssem.at[i, 6])

    held = {}

    def partner_a(k):
        onehots(p_src, pids, 4 * k, 512)
        onehots(p_dst.at[:, lanes[k]], pids, 16 + 4 * k, 512)
        h = dot(other_b[...], p_src[...])
        t = dot(own_b[...], p_dst[:, lanes[k]])
        q = complex_product(h, pr_s[:, lanes[k]])
        q_s[:, lanes[k]] = q
        g_pos = -jax.nn.sigmoid(-jnp.sum(q * t, axis=0, keepdims=True))
        for i, v in enumerate(split3(q * g_pos)):
            parts[400 * i : 400 * (i + 1), lanes[k]] = v

    def partner_b(k):
        q_b = q_s[:, lanes[k]].astype(bf16)
        gt[...] = (jax.nn.sigmoid(dot(own_b[...], q_b, 0, 0)) * 0.03125).astype(bf16)
        v = dot(q_b, gt[...], 1, 1) * counts(pids, 24 + 8 * k)
        dn[...] = v if k == 0 else dn[...] + v

    def dh(k):
        for i, v in enumerate(split3(conj_product(dq_s[:, lanes[k]], r_s[:, lanes[k]]))):
            dr3[400 * i : 400 * (i + 1), lanes[k]] = v

    def ent_scatter(n):
        rows = slice(256 * n, 256 * (n + 1))
        g = add3(dot(dr3[...], oh_src[rows, :], 1, 1) + dot(parts[...], p_dst[rows, :], 1, 1)) + dn[:, rows]
        for j in range(2):
            grad[2 * n + j] = g[:, 128 * j : 128 * (j + 1)].reshape(50, 8, 128)

    def ent(level):
        def push(src, dst, device):
            remote(src, dst, esend.at[level], erecv.at[level], device).start()

        if level == 0:
            for k in range(2):
                push(grad.at[2 * k + 1 - c], e0.at[k], near)
        elif level == 1:
            drain(e0, erecv.at[0])
            for k in range(2):
                hsum[k] = grad[2 * k + c] + e0[k]
            push(hsum.at[1 - zl], e1, far)
        elif level == 2:
            drain(e1, erecv.at[1])
            g = hsum[zl] + e1[...]
            square = jnp.sum(jnp.sum(g * g, axis=0), axis=0, keepdims=True)
            new_acc = acc[:, mine] + square * (1.0 / 400.0)
            nblk[m, 0:50] = emb[:, mine].reshape(50, 8, 128) - g * (learn_rate / jnp.sqrt(new_acc))
            nblk[m, 50] = jnp.broadcast_to(new_acc, (8, 128))
            push(nblk.at[m], nblk.at[m], far)
        elif level == 3:
            push(nblk.at[m], nblk.at[m], near)
        elif level == 4:
            drain(nblk.at[m], erecv.at[2])
            push(nblk.at[far_m], nblk.at[far_m], near)
        elif level == 5:
            drain(nblk.at[m], erecv.at[3])
            drain(nblk.at[m], erecv.at[4])
            for k in range(4):
                emb[:, 128 * k : 128 * (k + 1)] = nblk[k, 0:50].reshape(400, 128)
                acc[:, 128 * k : 128 * (k + 1)] = nblk[k, 50, 0:1]
            pltpu.make_async_copy(emb, nemb_out, osem.at[len(STREAMS)]).start()
            pltpu.make_async_copy(acc, nacc_out, osem.at[len(STREAMS) + 1]).start()
        else:
            drain(emb, osem.at[len(STREAMS)])
            drain(acc, osem.at[len(STREAMS) + 1])
            drain(e0, esend.at[0])
            drain(e1, esend.at[1])
            for k in range(2, 5):
                drain(nblk.at[m], esend.at[k])

    rel_scatter(0)
    step(0, 0)
    rel_scatter(1)
    step(1, 0)
    rel_scatter(2)
    step(2, 0)
    step(0, 1)
    rel_scatter(3)
    step(3, 0)
    step(1, 1)
    step(2, 1)
    step(3, 1)
    inputs[5].wait()
    partner_a(0)
    partner_b(0)
    partner_a(1)
    step(2, 2)
    partner_b(1)
    step(3, 2)
    step(0, 2)
    step(1, 2)
    dh(0)
    dh(1)
    ent_scatter(0)
    ent_scatter(1)
    ent(0)
    step(2, 3)
    step(0, 3)
    step(1, 3)
    step(3, 3)
    ent(1)
    for i in (2, 0, 1, 3):
        step(i, 4)
    ent(2)
    ent(3)
    for i in (0, 1, 2, 3):
        step(i, 5)
    ent(4)
    step(2, 6)
    step(0, 6)
    ent(5)
    step(1, 6)
    step(3, 6)
    for i in range(4):
        step(i, 7)
    ent(6)

    for copy in (a_far, a_near, a_fwd):
        copy.wait_send()
    drain(pay, send1)

    @pl.when(is_hub)
    def _():
        drain(stage, send2)


def bucket_round(*args):
    tile = lambda *lead: pltpu.VMEM((*lead, 16, 128), bf16)
    t = lambda *lead: pltpu.VMEM((*lead, 8, 128), f32)
    V = pltpu.VMEM
    dma = pltpu.SemaphoreType.DMA
    scratch = [
        V((1, 1024), i32), V((1, 1024), i32), V((1, 1024), i32), V((1, 2, 1024), i32), V((400, 512), f32),
        V((1, 512), f32), V((400, 1024), f32), dma((7,)),
        tile(32), tile(2, 64), tile(64), tile(32), tile(4, 25), t(4, 51),
        dma, dma, dma, dma, dma, dma, dma((3,)), dma((3,)),
        V((40, 128), i32), V((40, 128), i32), V((400, 512), bf16), V((400, 512), bf16), V((1200, 1024), bf16),
        V((512, 1024), bf16), V((512, 1024), bf16), V((1024, 1024), bf16),
        V((512, 512), bf16), V((512, 1024), bf16), V((1024, 512), bf16),
        V((400, 1024), f32), V((400, 1024), f32), V((400, 1024), f32), V((400, 1024), bf16), V((400, 1024), f32),
        V((400, 1024), f32), V((400, 1024), f32), V((8, 512), f32),
        V((1200, 1024), bf16), V((1200, 1024), bf16), V((512, 512), bf16), V((400, 512), f32),
        t(2, 200), t(4, 50),
        t(2, 50), t(50), t(2, 50), dma((5,)), dma((5,)), dma((len(STREAMS), 7)), dma((len(STREAMS), 7)), dma((len(STREAMS) + 2,)),
    ]
    for _, n, axes in STREAMS:
        scratch += stream_scratch(25 * n, axes)
    return pl.pallas_call(
        round_kernel,
        out_shape=(
            jax.ShapeDtypeStruct((2, 200, 8, 128), f32),
            jax.ShapeDtypeStruct((400, 512), f32),
            jax.ShapeDtypeStruct((1, 512), f32),
        ),
        in_specs=[ANY] * 7 + [SMEM] * 2,
        out_specs=(ANY, ANY, ANY),
        scratch_shapes=scratch,
        compiler_params=pltpu.CompilerParams(
            collective_id=1, has_side_effects=True, vmem_limit_bytes=56 * 2**20
        ),
        name="bucket_round",
    )(*args)


def update_kernel(
    total, nemb, nacc, rel_in, racc_in, nemb_out, nacc_out, nrel_out, nracc_out, g_v, rel_v, racc_v, emb_v, acc_v, sem
):
    copies = []

    def move(src, dst):
        copies.append(pltpu.make_async_copy(src, dst, sem.at[len(copies)]))
        copies[-1].start()
        return copies[-1]

    rows = [slice(0, 200), slice(200, 400)]
    fetch_g = [move(total.at[half], g_v.at[half]) for half in range(2)]
    fetch_racc = move(racc_in, racc_v)
    fetch_rel = [move(rel_in.at[rows[half]], rel_v.at[rows[half]]) for half in range(2)]
    fetch_ent = [move(nemb, emb_v), move(nacc, acc_v)]
    leave = []
    squares = [jnp.zeros((8, 128), f32)] * 8
    for half in range(2):
        fetch_g[half].wait()
        for k in range(8):
            for i in range(25):
                v = g_v[half, 25 * k + i]
                squares[k] = squares[k] + v * v
    for copy, src, dst in zip(fetch_ent, (emb_v, acc_v), (nemb_out, nacc_out)):
        copy.wait()
        leave.append(move(src, dst))
    fetch_racc.wait()
    rates = []
    for k in range(8):
        lanes = slice(128 * k, 128 * (k + 1))
        new_racc = racc_v[:, lanes] + jnp.sum(squares[k], axis=0, keepdims=True) * (1.0 / 400.0)
        rates.append(learn_rate / jnp.sqrt(new_racc))
        racc_v[:, lanes] = new_racc
    leave.append(move(racc_v, nracc_out))
    for half in range(2):
        fetch_rel[half].wait()
        for k in range(8):
            lanes = slice(128 * k, 128 * (k + 1))
            g = g_v[half, 25 * k : 25 * (k + 1)].reshape(200, 128)
            rel_v[rows[half], lanes] = rel_v[rows[half], lanes] - g * rates[k]
        leave.append(move(rel_v.at[rows[half]], nrel_out.at[rows[half]]))
    for copy in leave:
        copy.wait()


def update(total, nemb, nacc, relations, racc):
    shape = lambda *s: jax.ShapeDtypeStruct(s, f32)
    V = pltpu.VMEM
    return pl.pallas_call(
        update_kernel,
        out_shape=(shape(400, 512), shape(1, 512), shape(400, 1024), shape(1, 1024)),
        in_specs=[ANY] * 5,
        out_specs=(ANY,) * 4,
        scratch_shapes=[
            V((2, 200, 8, 128), f32), V((400, 1024), f32), V((1, 1024), f32),
            V((400, 512), f32), V((1, 512), f32), pltpu.SemaphoreType.DMA((12,)),
        ],
        compiler_params=pltpu.CompilerParams(vmem_limit_bytes=60 * 2**20),
        name="update",
    )(total, nemb, nacc, relations, racc)


def shards(embeddings, accum, relations, rel_accum, src_ids, rel_ids, dst_ids, neg_ids, bucket_len, partner):
    total, nemb, nacc = bucket_round(
        src_ids, rel_ids, dst_ids, neg_ids, embeddings, accum.reshape(1, 512), relations, bucket_len, partner
    )
    new_emb, new_acc, new_rel, new_racc = update(total, nemb, nacc, relations, rel_accum.reshape(1, 1024))
    return new_emb, new_acc.reshape(512), new_rel, new_racc.reshape(1024)


def solution(mesh):
    return jax.shard_map(
        shards,
        mesh=mesh,
        in_specs=(
            P(None, "dom"), P("dom"), P(), P(), P("dom", "edge"), P("dom", "edge"), P("dom", "edge"),
            P("dom", "edge", None), P("dom"), P(),
        ),
        out_specs=(P(None, "dom"), P("dom"), P(), P()),
        check_vma=False,
    )
```

```python
import jax
import jax.numpy as jnp
from jax import lax
from jax.experimental import pallas as pl
from jax.experimental.pallas import tpu as pltpu
from jax.sharding import PartitionSpec as P

MESH = pl.DeviceIdType.MESH
VMEM = pl.BlockSpec(memory_space=pltpu.VMEM)
SMEM = pl.BlockSpec(memory_space=pltpu.SMEM)
ANY = pl.BlockSpec(memory_space=pl.ANY)
f32, bf16, i32 = jnp.float32, jnp.bfloat16, jnp.int32
learn_rate = 0.1
HUBS = 32
ID_TILES = 5
SIZE = {"x": 4, "y": 8, "z": 8, "u": 8, "v": 8}
STREAMS = ((0, 2, 'yxz'), (2, 3, 'xyz'), (5, 3, 'xzy'))


def remote(src, dst, send, recv, device):
    return pltpu.make_async_remote_copy(
        src_ref=src, dst_ref=dst, send_sem=send, recv_sem=recv, device_id=device, device_id_type=MESH
    )


def drain(ref, sem):
    pltpu.make_async_copy(ref, ref, sem).wait()


def steps(size):
    return sorted(range(1, size), key=lambda s: (-min(s, size - s), s))


def levels(count, axes):
    n1 = -(-count // SIZE[axes[0]])
    return n1, -(-n1 // SIZE[axes[1]])


def stream_scratch(count, axes):
    n1, n2 = levels(count, axes)
    na, nb, nc = (SIZE[a] for a in axes)
    t = lambda *lead: pltpu.VMEM((*lead, 8, 128), f32)
    return [t(count), t(na * n1), t(na, n1), t(nb * n2), t(nb, n2), t(n2), t(nc, n2), t(nb * n2), t(na * n1)]


def onehots(out, ids, first, rows):
    for j in range(4):
        hit = lax.broadcasted_iota(i32, (rows, 128), 0) == ids[first + j : first + j + 1, :]
        out[:, 128 * j : 128 * (j + 1)] = jnp.where(hit, 1.0, 0.0).astype(bf16)


def split3(x):
    hi = x.astype(bf16)
    rest = x - hi.astype(f32)
    mid = rest.astype(bf16)
    lo = (rest - mid.astype(f32)).astype(bf16)
    return hi, mid, lo


def split2(x):
    hi = x.astype(bf16)
    return hi, (x - hi.astype(f32)).astype(bf16)


def dot(a, b, ca=1, cb=0):
    return lax.dot_general(a, b, (((ca,), (cb,)), ((), ())), preferred_element_type=f32)


def add3(x):
    return x[0:400] + x[400:800] + x[800:1200]


def add2(x):
    return x[0:400] + x[400:800]


def counts(ids, first):
    total = jnp.zeros((512, 128), f32)
    for j in range(8):
        hit = lax.broadcasted_iota(i32, (512, 128), 0) == ids[first + j : first + j + 1, :]
        total = total + jnp.where(hit, 1.0, 0.0)
    return dot(jnp.ones((8, 128), bf16), total.astype(bf16), 1, 1)[0:1]


def complex_product(a, b):
    return jnp.concatenate(
        [a[:200] * b[:200] - a[200:] * b[200:], a[:200] * b[200:] + a[200:] * b[:200]], axis=0
    )


def conj_product(a, b):
    return jnp.concatenate(
        [a[:200] * b[:200] + a[200:] * b[200:], a[200:] * b[:200] - a[:200] * b[200:]], axis=0
    )


def round_kernel(*refs):
    refs = list(refs)
    take = lambda n: [refs.pop(0) for _ in range(n)]
    src_in, rel_in, dst_in, neg_in, emb_in, acc_in, relations_in, len_ref, partner_ref = take(9)
    total, nemb_out, nacc_out = take(3)
    src_v, rel_v, dst_v, neg_v, emb, acc, relations, in_sem = take(8)
    pay, hub, stage, got, cols, nblk, send1, recv1, gsend, grecv, send2, recv2, asend, arecv = take(14)
    ids, pids, own_b, other_b, rel3, oh_src, oh_dst, oh_rel, p_src, p_dst, p_rel = take(11)
    h_s, r_s, q_s, qb_s, t_s, dq_s, pr_s, cnt, dr2, parts, gt, dn, grel, grad = take(14)
    e0, e1, hsum, esend, erecv, ssem, rsem, osem = take(8)
    streams = [(axes, 25 * n, 25 * lane, take(9)) for lane, n, axes in STREAMS]

    d, m = lax.axis_index("dom"), lax.axis_index("edge")
    zl, c = m // 2, m % 2
    zh, x, y = d // 32, d // 8 % 4, d % 8
    z = zh * 2 + zl
    at = lambda x, y, z: ((z // 2) * 32 + x * 8 + y, (z % 2) * 2 + c)
    far_m, near_m = (1 - zl) * 2 + c, zl * 2 + 1 - c
    far, near = (d, far_m), (d, near_m)
    spoke_m = (d + 3) % 4
    is_hub = (d // 8 + spoke_m) % 2 == zl
    order = lambda k: 2 + (k + 1) // 2 * (1 - 2 * (k % 2))

    def spoke(j):
        near_y, near_x, near_z = order(j // 4 % 4), order(j % 4), order(j // 16)
        return (zh + near_z) % 4 * 32 + (x + near_x) % 4 * 8 + (y // 2 + near_y) % 4 * 2 + c

    mine = pl.ds(pl.multiple_of(m * 128, 128), 128)
    place = {"x": x, "y": y, "z": z, "u": (1 - c) * y + c * z, "v": c * y + (1 - c) * z}
    peer = {
        "x": lambda s: at((x + s) % 4, y, z),
        "y": lambda s: at(x, (y + s) % 8, z),
        "z": lambda s: at(x, y, (z + s) % 8),
        "u": lambda s: at(x, (y + (1 - c) * s) % 8, (z + c * s) % 8),
        "v": lambda s: at(x, (y + c * s) % 8, (z + (1 - c) * s) % 8),
    }

    barrier = pltpu.get_barrier_semaphore()
    greet = lambda device: pl.semaphore_signal(barrier, inc=1, device_id=device, device_id_type=MESH)
    inputs = [
        pltpu.make_async_copy(a, b, in_sem.at[i])
        for i, (a, b) in enumerate(
            [(src_in, src_v), (rel_in, rel_v), (dst_in, dst_v), (neg_in, neg_v), (emb_in, emb), (acc_in, acc),
             (relations_in, relations)]
        )
    ]
    for copy in inputs:
        copy.start()

    def hello(j, _):
        greet((spoke(j), spoke_m))
        return 0

    @pl.when(is_hub)
    def _():
        lax.fori_loop(0, 64, hello, 0)

    greet(near)
    for axis in "xyz":
        for s in range(1, SIZE[axis]):
            greet(peer[axis](s))

    for copy in inputs[:5]:
        copy.wait()
    pay[0:25] = emb[:, mine].astype(bf16).reshape(25, 16, 128)
    slot = m * 1024 + lax.broadcasted_iota(i32, (8, 128), 0) * 128 + lax.broadcasted_iota(i32, (8, 128), 1)
    rows = [src_v, rel_v, dst_v, neg_v.at[0, 0:1], neg_v.at[0, 1:2]]
    for a, row in enumerate(rows):
        for j in range(8):
            ids[8 * a + j : 8 * a + j + 1, :] = row[0:1, 128 * j : 128 * (j + 1)]
        v = ids[8 * a : 8 * a + 8, :]
        if a == 0:
            v = jnp.where(slot < len_ref[0], v, 512)
            ids[0:8, :] = v
        pay[25 + a] = jnp.concatenate([(v >> 5).astype(f32), (v & 31).astype(f32)], axis=0).astype(bf16)
    pay[30:32] = jnp.zeros((2, 16, 128), bf16)
    pl.semaphore_wait(barrier, HUBS + 18)

    def leg1(i, _):
        i = (zh + order(i // 8)) % 4 * 8 + (x + order(i % 4)) % 4 * 2 + (y // 4 + 1 + i // 4) % 2
        device = (4 * i + (m + 1) % 4, (i // 2 + m) % 2 * 2 + d % 2)
        remote(pay.at[i], hub.at[d % 2, d // 2], send1, recv1, device).start()
        return 0

    lax.fori_loop(0, HUBS, leg1, 0)

    lanes = [slice(0, 512), slice(512, 1024)]

    def gather_rel(hot, ids, k, out):
        onehots(hot, ids, 8 + 4 * k, 1024)
        out[:, lanes[k]] = add3(dot(rel3[...], hot[...]))

    def own_start(k):
        onehots(oh_src.at[:, lanes[k]], ids, 4 * k, 512)
        h = dot(own_b[...], oh_src[:, lanes[k]])
        h_s[:, lanes[k]] = h
        q = complex_product(h, r_s[:, lanes[k]])
        q_s[:, lanes[k]] = q
        qb_s[:, lanes[k]] = q.astype(bf16)
        onehots(oh_dst.at[:, lanes[k]], ids, 16 + 4 * k, 512)

    own_b[...] = emb[...].astype(bf16)
    inputs[6].wait()
    rel3[0:400], rel3[400:800], rel3[800:1200] = split3(relations[...])
    gather_rel(oh_rel.at[:, lanes[0]], ids, 0, r_s)

    def leg2(j, _):
        t = spoke(j)
        p = partner_ref[t]
        stage[j] = hub[p % 2, p // 2]
        remote(stage.at[j], got.at[d // 4], send2, recv2, (t, spoke_m)).start()
        return 0

    @pl.when(is_hub)
    def _():
        drain(hub.at[c], recv1)
        share = remote(hub.at[c], hub.at[c], gsend, grecv, near)
        share.start()
        share.wait()
        lax.fori_loop(0, 64, leg2, 0)

    gather_rel(oh_rel.at[:, lanes[1]], ids, 1, r_s)
    own_start(0)
    own_start(1)
    for k in range(2):
        cnt[k : k + 1, :] = counts(ids, 24 + 8 * k)
    drain(got, recv2)

    block = got.at[pl.ds(0, 25)]
    a_far = remote(block, cols.at[m], asend.at[0], arecv.at[0], far)
    a_near = remote(block, cols.at[m], asend.at[1], arecv.at[1], near)
    a_far.start()
    a_near.start()

    def place_cols(k, value):
        other_b[:, pl.ds(pl.multiple_of(k * 128, 128), 128)] = value.reshape(400, 128)

    def own_part(k, pair):
        ents = pl.ds(pl.multiple_of(pair * 256, 256), 256)
        part = other_b[:, ents]
        t = dot(part, oh_dst[ents, lanes[k]])
        negs = dot(part, qb_s[:, lanes[k]], 0, 0)
        g = (jax.nn.sigmoid(negs) * 0.03125).astype(bf16)
        weighted = part.astype(f32) * cnt[k : k + 1, ents]
        w_hi = weighted.astype(bf16)
        w_lo = (weighted - w_hi.astype(f32)).astype(bf16)
        return t, dot(w_hi, g) + dot(w_lo, g)

    place_cols(m, got[0:25])
    cols[m] = got[0:25]
    for a in range(ID_TILES):
        v = got[25 + a].astype(f32)
        pids[8 * a : 8 * a + 8, :] = (v[:8] * 32.0 + v[8:]).astype(i32)
    gather_rel(p_rel, pids, 0, pr_s)
    a_near.wait_recv()
    place_cols(near_m, cols[near_m])
    for k in range(2):
        t_s[:, lanes[k]], dq_s[:, lanes[k]] = own_part(k, zl)
    a_far.wait_recv()
    a_fwd = remote(cols.at[far_m], cols.at[far_m], asend.at[2], arecv.at[2], near)
    a_fwd.start()
    place_cols(far_m, cols[far_m])
    gather_rel(p_rel, pids, 1, pr_s)
    a_fwd.wait_recv()
    place_cols(3 - m, cols[3 - m])

    for k in range(2):
        t, back = own_part(k, 1 - zl)
        t = t + t_s[:, lanes[k]]
        g_pos = -jax.nn.sigmoid(-jnp.sum(q_s[:, lanes[k]] * t, axis=0, keepdims=True))
        dq = t * g_pos + (dq_s[:, lanes[k]] + back)
        dq_s[:, lanes[k]] = dq
        for i, v in enumerate(split2(conj_product(dq, h_s[:, lanes[k]]))):
            dr2[400 * i : 400 * (i + 1), lanes[k]] = v

    def rel_scatter(n):
        g = add2(dot(dr2[...], oh_rel[256 * n : 256 * (n + 1), :], 1, 1))
        for j in range(2):
            for half in range(2):
                grel[half, pl.ds(25 * (2 * n + j), 25)] = g[
                    200 * half : 200 * (half + 1), 128 * j : 128 * (j + 1)
                ].reshape(25, 8, 128)

    def step(i, level):
        axes, T, base, (in0, a, in1, b, in2, last, in3, gb, ga) = streams[i]
        n1, n2 = levels(T, axes)
        (A, B, C), (na, nb, nc) = axes, [SIZE[k] for k in axes]
        ma, mb, mc = place[A], place[B], place[C]
        zeros = lambda n: jnp.zeros((n, 8, 128), f32)

        def push(src, dst, device):
            remote(src, dst, ssem.at[i, level], rsem.at[i, level], device).start()

        if level == 0:
            push(grel.at[1 - c, pl.ds(base, T)], in0, near)
        elif level == 1:
            drain(in0, rsem.at[i, 0])
            a[0:T] = grel[c, pl.ds(base, T)] + in0[...]
            if na * n1 > T:
                a[T : na * n1] = zeros(na * n1 - T)
            for s in steps(na):
                push(a.at[pl.ds(n1 * ((ma + s) % na), n1)], in1.at[ma], peer[A](s))
        elif level == 2:
            drain(in1.at[pl.ds(0, na - 1)], rsem.at[i, 1])
            v = a[pl.ds(n1 * ma, n1)]
            for s in range(1, na):
                v = v + in1[(ma + s) % na]
            b[0:n1] = v
            if nb * n2 > n1:
                b[n1 : nb * n2] = zeros(nb * n2 - n1)
            for s in steps(nb):
                push(b.at[pl.ds(n2 * ((mb + s) % nb), n2)], in2.at[mb], peer[B](s))
        elif level == 3:
            drain(in2.at[pl.ds(0, nb - 1)], rsem.at[i, 2])
            v = b[pl.ds(n2 * mb, n2)]
            for s in range(1, nb):
                v = v + in2[(mb + s) % nb]
            last[...] = v
            in3[mc] = v
            for s in steps(nc):
                push(last, in3.at[mc], peer[C](s))
        elif level == 4:
            drain(in3.at[pl.ds(0, nc - 1)], rsem.at[i, 3])
            v = in3[0]
            for s in range(1, nc):
                v = v + in3[s]
            spot = pl.ds(n2 * mb, n2)
            gb[spot] = v
            for s in steps(nb):
                push(gb.at[spot], gb.at[spot], peer[B](s))
        elif level == 5:
            drain(gb.at[pl.ds(0, (nb - 1) * n2)], rsem.at[i, 4])
            spot = pl.ds(n1 * ma, n1)
            for s in steps(na):
                push(gb.at[pl.ds(0, n1)], ga.at[spot], peer[A](s))
            ga[spot] = gb[0:n1]
        elif level == 6:
            drain(ga.at[pl.ds(0, (na - 1) * n1)], rsem.at[i, 5])
            push(ga.at[pl.ds(0, T)], total.at[c, pl.ds(base, T)], near)
            pltpu.make_async_copy(ga.at[pl.ds(0, T)], total.at[c, pl.ds(base, T)], osem.at[i]).start()
        else:
            drain(in0, osem.at[i])
            drain(in0, rsem.at[i, 6])
            drain(in0, ssem.at[i, 0])
            drain(in1.at[pl.ds(0, na - 1)], ssem.at[i, 1])
            drain(in2.at[pl.ds(0, nb - 1)], ssem.at[i, 2])
            drain(in3.at[pl.ds(0, nc - 1)], ssem.at[i, 3])
            drain(gb.at[pl.ds(0, (nb - 1) * n2)], ssem.at[i, 4])
            drain(ga.at[pl.ds(0, (na - 1) * n1)], ssem.at[i, 5])
            drain(in0, ssem.at[i, 6])

    held = {}

    def partner_a(k):
        onehots(p_src, pids, 4 * k, 512)
        onehots(p_dst.at[:, lanes[k]], pids, 16 + 4 * k, 512)
        h = dot(other_b[...], p_src[...])
        t = dot(own_b[...], p_dst[:, lanes[k]])
        q = complex_product(h, pr_s[:, lanes[k]])
        q_s[:, lanes[k]] = q
        g_pos = -jax.nn.sigmoid(-jnp.sum(q * t, axis=0, keepdims=True))
        for i, v in enumerate(split2(q * g_pos)):
            parts[400 * i : 400 * (i + 1), lanes[k]] = v

    def partner_b(k):
        q_b = q_s[:, lanes[k]].astype(bf16)
        gt[...] = (jax.nn.sigmoid(dot(own_b[...], q_b, 0, 0)) * 0.03125).astype(bf16)
        v = dot(q_b, gt[...], 1, 1) * counts(pids, 24 + 8 * k)
        dn[...] = v if k == 0 else dn[...] + v

    def dh(k):
        for i, v in enumerate(split2(conj_product(dq_s[:, lanes[k]], r_s[:, lanes[k]]))):
            dr2[400 * i : 400 * (i + 1), lanes[k]] = v

    def ent_scatter(n):
        rows = slice(256 * n, 256 * (n + 1))
        g = add2(dot(dr2[...], oh_src[rows, :], 1, 1) + dot(parts[...], p_dst[rows, :], 1, 1)) + dn[:, rows]
        for j in range(2):
            grad[2 * n + j] = g[:, 128 * j : 128 * (j + 1)].reshape(50, 8, 128)

    def ent(level):
        def push(src, dst, device):
            remote(src, dst, esend.at[level], erecv.at[level], device).start()

        if level == 0:
            for k in range(2):
                push(grad.at[2 * k + 1 - c], e0.at[k], near)
        elif level == 1:
            drain(e0, erecv.at[0])
            for k in range(2):
                hsum[k] = grad[2 * k + c] + e0[k]
            push(hsum.at[1 - zl], e1, far)
        elif level == 2:
            drain(e1, erecv.at[1])
            g = hsum[zl] + e1[...]
            square = jnp.sum(jnp.sum(g * g, axis=0), axis=0, keepdims=True)
            new_acc = acc[:, mine] + square * (1.0 / 400.0)
            nblk[m, 0:50] = emb[:, mine].reshape(50, 8, 128) - g * (learn_rate / jnp.sqrt(new_acc))
            nblk[m, 50] = jnp.broadcast_to(new_acc, (8, 128))
            push(nblk.at[m], nblk.at[m], far)
        elif level == 3:
            push(nblk.at[m], nblk.at[m], near)
        elif level == 4:
            drain(nblk.at[m], erecv.at[2])
            push(nblk.at[far_m], nblk.at[far_m], near)
        elif level == 5:
            drain(nblk.at[m], erecv.at[3])
            drain(nblk.at[m], erecv.at[4])
            for k in range(4):
                emb[:, 128 * k : 128 * (k + 1)] = nblk[k, 0:50].reshape(400, 128)
                acc[:, 128 * k : 128 * (k + 1)] = nblk[k, 50, 0:1]
            pltpu.make_async_copy(emb, nemb_out, osem.at[len(STREAMS)]).start()
            pltpu.make_async_copy(acc, nacc_out, osem.at[len(STREAMS) + 1]).start()
        else:
            drain(emb, osem.at[len(STREAMS)])
            drain(acc, osem.at[len(STREAMS) + 1])
            drain(e0, esend.at[0])
            drain(e1, esend.at[1])
            for k in range(2, 5):
                drain(nblk.at[m], esend.at[k])

    rel_scatter(0)
    step(0, 0)
    rel_scatter(1)
    rel_scatter(2)
    step(1, 0)
    step(0, 1)
    rel_scatter(3)
    step(2, 0)
    step(1, 1)
    step(2, 1)
    inputs[5].wait()
    partner_a(0)
    partner_b(0)
    partner_a(1)
    step(1, 2)
    partner_b(1)
    step(2, 2)
    step(0, 2)
    dh(0)
    dh(1)
    ent_scatter(0)
    ent_scatter(1)
    ent(0)
    step(1, 3)
    step(0, 3)
    step(2, 3)
    ent(1)
    step(1, 4)
    step(0, 4)
    step(2, 4)
    ent(2)
    ent(3)
    step(0, 5)
    step(1, 5)
    step(2, 5)
    ent(4)
    step(1, 6)
    step(0, 6)
    ent(5)
    step(2, 6)
    for i in range(3):
        step(i, 7)
    ent(6)

    for copy in (a_far, a_near, a_fwd):
        copy.wait_send()
    drain(pay, send1)

    @pl.when(is_hub)
    def _():
        drain(stage, send2)


def bucket_round(*args):
    tile = lambda *lead: pltpu.VMEM((*lead, 16, 128), bf16)
    t = lambda *lead: pltpu.VMEM((*lead, 8, 128), f32)
    V = pltpu.VMEM
    dma = pltpu.SemaphoreType.DMA
    scratch = [
        V((1, 1024), i32), V((1, 1024), i32), V((1, 1024), i32), V((1, 2, 1024), i32), V((400, 512), f32),
        V((1, 512), f32), V((400, 1024), f32), dma((7,)),
        tile(32), tile(2, 64), tile(64), tile(32), tile(4, 25), t(4, 51),
        dma, dma, dma, dma, dma, dma, dma((3,)), dma((3,)),
        V((40, 128), i32), V((40, 128), i32), V((400, 512), bf16), V((400, 512), bf16), V((1200, 1024), bf16),
        V((512, 1024), bf16), V((512, 1024), bf16), V((1024, 1024), bf16),
        V((512, 512), bf16), V((512, 1024), bf16), V((1024, 512), bf16),
        V((400, 1024), f32), V((400, 1024), f32), V((400, 1024), f32), V((400, 1024), bf16), V((400, 1024), f32),
        V((400, 1024), f32), V((400, 1024), f32), V((8, 512), f32),
        V((800, 1024), bf16), V((800, 1024), bf16), V((512, 512), bf16), V((400, 512), f32),
        t(2, 200), t(4, 50),
        t(2, 50), t(50), t(2, 50), dma((5,)), dma((5,)), dma((len(STREAMS), 7)), dma((len(STREAMS), 7)), dma((len(STREAMS) + 2,)),
    ]
    for _, n, axes in STREAMS:
        scratch += stream_scratch(25 * n, axes)
    return pl.pallas_call(
        round_kernel,
        out_shape=(
            jax.ShapeDtypeStruct((2, 200, 8, 128), f32),
            jax.ShapeDtypeStruct((400, 512), f32),
            jax.ShapeDtypeStruct((1, 512), f32),
        ),
        in_specs=[ANY] * 7 + [SMEM] * 2,
        out_specs=(ANY, ANY, ANY),
        scratch_shapes=scratch,
        compiler_params=pltpu.CompilerParams(
            collective_id=1, has_side_effects=True, vmem_limit_bytes=56 * 2**20
        ),
        name="bucket_round",
    )(*args)


def update_kernel(
    total, nemb, nacc, rel_in, racc_in, nemb_out, nacc_out, nrel_out, nracc_out, g_v, rel_v, racc_v, emb_v, acc_v, sem
):
    copies = []

    def move(src, dst):
        copies.append(pltpu.make_async_copy(src, dst, sem.at[len(copies)]))
        copies[-1].start()
        return copies[-1]

    rows = [slice(0, 200), slice(200, 400)]
    fetch_g = [move(total.at[half], g_v.at[half]) for half in range(2)]
    fetch_racc = move(racc_in, racc_v)
    fetch_rel = [move(rel_in.at[rows[half]], rel_v.at[rows[half]]) for half in range(2)]
    fetch_ent = [move(nemb, emb_v), move(nacc, acc_v)]
    leave = []
    squares = [jnp.zeros((8, 128), f32)] * 8
    for half in range(2):
        fetch_g[half].wait()
        for k in range(8):
            for i in range(25):
                v = g_v[half, 25 * k + i]
                squares[k] = squares[k] + v * v
    for copy, src, dst in zip(fetch_ent, (emb_v, acc_v), (nemb_out, nacc_out)):
        copy.wait()
        leave.append(move(src, dst))
    fetch_racc.wait()
    rates = []
    for k in range(8):
        lanes = slice(128 * k, 128 * (k + 1))
        new_racc = racc_v[:, lanes] + jnp.sum(squares[k], axis=0, keepdims=True) * (1.0 / 400.0)
        rates.append(learn_rate / jnp.sqrt(new_racc))
        racc_v[:, lanes] = new_racc
    leave.append(move(racc_v, nracc_out))
    for half in range(2):
        fetch_rel[half].wait()
        for k in range(8):
            lanes = slice(128 * k, 128 * (k + 1))
            g = g_v[half, 25 * k : 25 * (k + 1)].reshape(200, 128)
            rel_v[rows[half], lanes] = rel_v[rows[half], lanes] - g * rates[k]
        leave.append(move(rel_v.at[rows[half]], nrel_out.at[rows[half]]))
    for copy in leave:
        copy.wait()


def update(total, nemb, nacc, relations, racc):
    shape = lambda *s: jax.ShapeDtypeStruct(s, f32)
    V = pltpu.VMEM
    return pl.pallas_call(
        update_kernel,
        out_shape=(shape(400, 512), shape(1, 512), shape(400, 1024), shape(1, 1024)),
        in_specs=[ANY] * 5,
        out_specs=(ANY,) * 4,
        scratch_shapes=[
            V((2, 200, 8, 128), f32), V((400, 1024), f32), V((1, 1024), f32),
            V((400, 512), f32), V((1, 512), f32), pltpu.SemaphoreType.DMA((12,)),
        ],
        compiler_params=pltpu.CompilerParams(vmem_limit_bytes=60 * 2**20),
        name="update",
    )(total, nemb, nacc, relations, racc)


def shards(embeddings, accum, relations, rel_accum, src_ids, rel_ids, dst_ids, neg_ids, bucket_len, partner):
    total, nemb, nacc = bucket_round(
        src_ids, rel_ids, dst_ids, neg_ids, embeddings, accum.reshape(1, 512), relations, bucket_len, partner
    )
    new_emb, new_acc, new_rel, new_racc = update(total, nemb, nacc, relations, rel_accum.reshape(1, 1024))
    return new_emb, new_acc.reshape(512), new_rel, new_racc.reshape(1024)


def solution(mesh):
    return jax.shard_map(
        shards,
        mesh=mesh,
        in_specs=(
            P(None, "dom"), P("dom"), P(), P(), P("dom", "edge"), P("dom", "edge"), P("dom", "edge"),
            P("dom", "edge", None), P("dom"), P(),
        ),
        out_specs=(P(None, "dom"), P("dom"), P(), P()),
        check_vma=False,
    )
```

```python
import jax
import jax.numpy as jnp
from jax import lax
from jax.experimental import pallas as pl
from jax.experimental.pallas import tpu as pltpu
from jax.sharding import PartitionSpec as P

MESH = pl.DeviceIdType.MESH
VMEM = pl.BlockSpec(memory_space=pltpu.VMEM)
SMEM = pl.BlockSpec(memory_space=pltpu.SMEM)
ANY = pl.BlockSpec(memory_space=pl.ANY)
f32, bf16, i32 = jnp.float32, jnp.bfloat16, jnp.int32
learn_rate = 0.1
HUBS = 32
ID_TILES = 5
SIZE = {"x": 4, "y": 8, "z": 8, "u": 8, "v": 8}
STREAMS = ((0, 3, 'xyz'), (3, 3, 'xzy'), (6, 2, 'yxz'))


def remote(src, dst, send, recv, device):
    return pltpu.make_async_remote_copy(
        src_ref=src, dst_ref=dst, send_sem=send, recv_sem=recv, device_id=device, device_id_type=MESH
    )


def drain(ref, sem):
    pltpu.make_async_copy(ref, ref, sem).wait()


def steps(size):
    return sorted(range(1, size), key=lambda s: (-min(s, size - s), s))


def levels(count, axes):
    n1 = -(-count // SIZE[axes[0]])
    return n1, -(-n1 // SIZE[axes[1]])


def stream_scratch(count, axes):
    n1, n2 = levels(count, axes)
    na, nb, nc = (SIZE[a] for a in axes)
    t = lambda *lead: pltpu.VMEM((*lead, 8, 128), f32)
    return [t(count), t(na * n1), t(na, n1), t(nb * n2), t(nb, n2), t(n2), t(nc, n2), t(nb * n2), t(na * n1)]


def onehots(out, ids, first, rows):
    for j in range(4):
        hit = lax.broadcasted_iota(i32, (rows, 128), 0) == ids[first + j : first + j + 1, :]
        out[:, 128 * j : 128 * (j + 1)] = jnp.where(hit, 1.0, 0.0).astype(bf16)


def split3(x):
    hi = x.astype(bf16)
    rest = x - hi.astype(f32)
    mid = rest.astype(bf16)
    lo = (rest - mid.astype(f32)).astype(bf16)
    return hi, mid, lo


def split2(x):
    hi = x.astype(bf16)
    return hi, (x - hi.astype(f32)).astype(bf16)


def dot(a, b, ca=1, cb=0):
    return lax.dot_general(a, b, (((ca,), (cb,)), ((), ())), preferred_element_type=f32)


def add3(x):
    return x[0:400] + x[400:800] + x[800:1200]


def add2(x):
    return x[0:400] + x[400:800]


def counts(ids, first):
    total = jnp.zeros((512, 128), f32)
    for j in range(8):
        hit = lax.broadcasted_iota(i32, (512, 128), 0) == ids[first + j : first + j + 1, :]
        total = total + jnp.where(hit, 1.0, 0.0)
    return dot(jnp.ones((8, 128), bf16), total.astype(bf16), 1, 1)[0:1]


def complex_product(a, b):
    return jnp.concatenate(
        [a[:200] * b[:200] - a[200:] * b[200:], a[:200] * b[200:] + a[200:] * b[:200]], axis=0
    )


def conj_product(a, b):
    return jnp.concatenate(
        [a[:200] * b[:200] + a[200:] * b[200:], a[200:] * b[:200] - a[:200] * b[200:]], axis=0
    )


def round_kernel(*refs):
    refs = list(refs)
    take = lambda n: [refs.pop(0) for _ in range(n)]
    src_in, rel_in, dst_in, neg_in, emb_in, acc_in, relations_in, len_ref, partner_ref = take(9)
    total, nemb_out, nacc_out = take(3)
    src_v, rel_v, dst_v, neg_v, emb, acc, relations, in_sem = take(8)
    pay, hub, stage, got, cols, nblk, send1, recv1, gsend, grecv, send2, recv2, asend, arecv = take(14)
    ids, pids, own_b, other_b, rel3, oh_src, oh_dst, oh_rel, p_src, p_dst, p_rel = take(11)
    h_s, r_s, q_s, qb_s, t_s, dq_s, pr_s, cnt, dr2, parts, gt, dn, grel, grad = take(14)
    e0, e1, hsum, esend, erecv, ssem, rsem, osem = take(8)
    streams = [(axes, 25 * n, 25 * lane, take(9)) for lane, n, axes in STREAMS]

    d, m = lax.axis_index("dom"), lax.axis_index("edge")
    zl, c = m // 2, m % 2
    zh, x, y = d // 32, d // 8 % 4, d % 8
    z = zh * 2 + zl
    at = lambda x, y, z: ((z // 2) * 32 + x * 8 + y, (z % 2) * 2 + c)
    far_m, near_m = (1 - zl) * 2 + c, zl * 2 + 1 - c
    far, near = (d, far_m), (d, near_m)
    spoke_m = (d + 3) % 4
    is_hub = (d // 8 + spoke_m) % 2 == zl
    order = lambda k: 2 + (k + 1) // 2 * (1 - 2 * (k % 2))

    def spoke(j):
        near_y, near_x, near_z = order(j // 4 % 4), order(j % 4), order(j // 16)
        return (zh + near_z) % 4 * 32 + (x + near_x) % 4 * 8 + (y // 2 + near_y) % 4 * 2 + c

    mine = pl.ds(pl.multiple_of(m * 128, 128), 128)
    place = {"x": x, "y": y, "z": z, "u": (1 - c) * y + c * z, "v": c * y + (1 - c) * z}
    peer = {
        "x": lambda s: at((x + s) % 4, y, z),
        "y": lambda s: at(x, (y + s) % 8, z),
        "z": lambda s: at(x, y, (z + s) % 8),
        "u": lambda s: at(x, (y + (1 - c) * s) % 8, (z + c * s) % 8),
        "v": lambda s: at(x, (y + c * s) % 8, (z + (1 - c) * s) % 8),
    }

    barrier = pltpu.get_barrier_semaphore()
    greet = lambda device: pl.semaphore_signal(barrier, inc=1, device_id=device, device_id_type=MESH)
    inputs = [
        pltpu.make_async_copy(a, b, in_sem.at[i])
        for i, (a, b) in enumerate(
            [(src_in, src_v), (rel_in, rel_v), (dst_in, dst_v), (neg_in, neg_v), (emb_in, emb), (acc_in, acc),
             (relations_in, relations)]
        )
    ]
    for copy in inputs:
        copy.start()

    def hello(j, _):
        greet((spoke(j), spoke_m))
        return 0

    @pl.when(is_hub)
    def _():
        lax.fori_loop(0, 64, hello, 0)

    greet(near)
    for axis in "xyz":
        for s in range(1, SIZE[axis]):
            greet(peer[axis](s))

    for copy in inputs[:5]:
        copy.wait()
    pay[0:25] = emb[:, mine].astype(bf16).reshape(25, 16, 128)
    slot = m * 1024 + lax.broadcasted_iota(i32, (8, 128), 0) * 128 + lax.broadcasted_iota(i32, (8, 128), 1)
    rows = [src_v, rel_v, dst_v, neg_v.at[0, 0:1], neg_v.at[0, 1:2]]
    for a, row in enumerate(rows):
        for j in range(8):
            ids[8 * a + j : 8 * a + j + 1, :] = row[0:1, 128 * j : 128 * (j + 1)]
        v = ids[8 * a : 8 * a + 8, :]
        if a == 0:
            v = jnp.where(slot < len_ref[0], v, 512)
            ids[0:8, :] = v
        pay[25 + a] = jnp.concatenate([(v >> 5).astype(f32), (v & 31).astype(f32)], axis=0).astype(bf16)
    pay[30:32] = jnp.zeros((2, 16, 128), bf16)
    pl.semaphore_wait(barrier, HUBS + 18)

    def leg1(i, _):
        i = (zh + order(i // 8)) % 4 * 8 + (x + order(i % 4)) % 4 * 2 + (y // 4 + 1 + i // 4) % 2
        device = (4 * i + (m + 1) % 4, (i // 2 + m) % 2 * 2 + d % 2)
        remote(pay.at[i], hub.at[d % 2, d // 2], send1, recv1, device).start()
        return 0

    lax.fori_loop(0, HUBS, leg1, 0)

    lanes = [slice(0, 512), slice(512, 1024)]

    def gather_rel(hot, ids, k, out):
        onehots(hot, ids, 8 + 4 * k, 1024)
        out[:, lanes[k]] = add3(dot(rel3[...], hot[...]))

    def own_start(k):
        onehots(oh_src.at[:, lanes[k]], ids, 4 * k, 512)
        h = dot(own_b[...], oh_src[:, lanes[k]])
        h_s[:, lanes[k]] = h
        q = complex_product(h, r_s[:, lanes[k]])
        q_s[:, lanes[k]] = q
        qb_s[:, lanes[k]] = q.astype(bf16)
        onehots(oh_dst.at[:, lanes[k]], ids, 16 + 4 * k, 512)

    own_b[...] = emb[...].astype(bf16)
    inputs[6].wait()
    rel3[0:400], rel3[400:800], rel3[800:1200] = split3(relations[...])
    gather_rel(oh_rel.at[:, lanes[0]], ids, 0, r_s)
    own_start(0)

    def leg2(j, _):
        t = spoke(j)
        p = partner_ref[t]
        stage[j] = hub[p % 2, p // 2]
        remote(stage.at[j], got.at[d // 4], send2, recv2, (t, spoke_m)).start()
        return 0

    @pl.when(is_hub)
    def _():
        drain(hub.at[c], recv1)
        share = remote(hub.at[c], hub.at[c], gsend, grecv, near)
        share.start()
        share.wait()
        lax.fori_loop(0, 64, leg2, 0)

    gather_rel(oh_rel.at[:, lanes[1]], ids, 1, r_s)
    own_start(1)
    for k in range(2):
        cnt[k : k + 1, :] = counts(ids, 24 + 8 * k)
    drain(got, recv2)

    block = got.at[pl.ds(0, 25)]
    a_far = remote(block, cols.at[m], asend.at[0], arecv.at[0], far)
    a_near = remote(block, cols.at[m], asend.at[1], arecv.at[1], near)
    a_far.start()
    a_near.start()

    def place_cols(k, value):
        other_b[:, pl.ds(pl.multiple_of(k * 128, 128), 128)] = value.reshape(400, 128)

    def own_part(k, pair):
        ents = pl.ds(pl.multiple_of(pair * 256, 256), 256)
        part = other_b[:, ents]
        t = dot(part, oh_dst[ents, lanes[k]])
        negs = dot(part, qb_s[:, lanes[k]], 0, 0)
        g = (jax.nn.sigmoid(negs) * 0.03125).astype(bf16)
        weighted = part.astype(f32) * cnt[k : k + 1, ents]
        w_hi = weighted.astype(bf16)
        w_lo = (weighted - w_hi.astype(f32)).astype(bf16)
        return t, dot(w_hi, g) + dot(w_lo, g)

    place_cols(m, got[0:25])
    cols[m] = got[0:25]
    for a in range(ID_TILES):
        v = got[25 + a].astype(f32)
        pids[8 * a : 8 * a + 8, :] = (v[:8] * 32.0 + v[8:]).astype(i32)
    gather_rel(p_rel, pids, 0, pr_s)
    a_near.wait_recv()
    place_cols(near_m, cols[near_m])
    for k in range(2):
        t_s[:, lanes[k]], dq_s[:, lanes[k]] = own_part(k, zl)
    a_far.wait_recv()
    a_fwd = remote(cols.at[far_m], cols.at[far_m], asend.at[2], arecv.at[2], near)
    a_fwd.start()
    place_cols(far_m, cols[far_m])
    gather_rel(p_rel, pids, 1, pr_s)
    a_fwd.wait_recv()
    place_cols(3 - m, cols[3 - m])

    for k in range(2):
        t, back = own_part(k, 1 - zl)
        t = t + t_s[:, lanes[k]]
        g_pos = -jax.nn.sigmoid(-jnp.sum(q_s[:, lanes[k]] * t, axis=0, keepdims=True))
        dq = t * g_pos + (dq_s[:, lanes[k]] + back)
        dq_s[:, lanes[k]] = dq
        for i, v in enumerate(split2(conj_product(dq, h_s[:, lanes[k]]))):
            dr2[400 * i : 400 * (i + 1), lanes[k]] = v

    def rel_scatter(n):
        g = add2(dot(dr2[...], oh_rel[256 * n : 256 * (n + 1), :], 1, 1))
        for j in range(2):
            for half in range(2):
                grel[half, pl.ds(25 * (2 * n + j), 25)] = g[
                    200 * half : 200 * (half + 1), 128 * j : 128 * (j + 1)
                ].reshape(25, 8, 128)

    def step(i, level):
        axes, T, base, (in0, a, in1, b, in2, last, in3, gb, ga) = streams[i]
        n1, n2 = levels(T, axes)
        (A, B, C), (na, nb, nc) = axes, [SIZE[k] for k in axes]
        ma, mb, mc = place[A], place[B], place[C]
        zeros = lambda n: jnp.zeros((n, 8, 128), f32)

        def push(src, dst, device):
            remote(src, dst, ssem.at[i, level], rsem.at[i, level], device).start()

        if level == 0:
            push(grel.at[1 - c, pl.ds(base, T)], in0, near)
        elif level == 1:
            drain(in0, rsem.at[i, 0])
            a[0:T] = grel[c, pl.ds(base, T)] + in0[...]
            if na * n1 > T:
                a[T : na * n1] = zeros(na * n1 - T)
            for s in steps(na):
                push(a.at[pl.ds(n1 * ((ma + s) % na), n1)], in1.at[ma], peer[A](s))
        elif level == 2:
            drain(in1.at[pl.ds(0, na - 1)], rsem.at[i, 1])
            v = a[pl.ds(n1 * ma, n1)]
            for s in range(1, na):
                v = v + in1[(ma + s) % na]
            b[0:n1] = v
            if nb * n2 > n1:
                b[n1 : nb * n2] = zeros(nb * n2 - n1)
            for s in steps(nb):
                push(b.at[pl.ds(n2 * ((mb + s) % nb), n2)], in2.at[mb], peer[B](s))
        elif level == 3:
            drain(in2.at[pl.ds(0, nb - 1)], rsem.at[i, 2])
            v = b[pl.ds(n2 * mb, n2)]
            for s in range(1, nb):
                v = v + in2[(mb + s) % nb]
            last[...] = v
            in3[mc] = v
            for s in steps(nc):
                push(last, in3.at[mc], peer[C](s))
        elif level == 4:
            drain(in3.at[pl.ds(0, nc - 1)], rsem.at[i, 3])
            v = in3[0]
            for s in range(1, nc):
                v = v + in3[s]
            spot = pl.ds(n2 * mb, n2)
            gb[spot] = v
            for s in steps(nb):
                push(gb.at[spot], gb.at[spot], peer[B](s))
        elif level == 5:
            drain(gb.at[pl.ds(0, (nb - 1) * n2)], rsem.at[i, 4])
            spot = pl.ds(n1 * ma, n1)
            for s in steps(na):
                push(gb.at[pl.ds(0, n1)], ga.at[spot], peer[A](s))
            ga[spot] = gb[0:n1]
        elif level == 6:
            drain(ga.at[pl.ds(0, (na - 1) * n1)], rsem.at[i, 5])
            push(ga.at[pl.ds(0, T)], total.at[c, pl.ds(base, T)], near)
            pltpu.make_async_copy(ga.at[pl.ds(0, T)], total.at[c, pl.ds(base, T)], osem.at[i]).start()
        else:
            drain(in0, osem.at[i])
            drain(in0, rsem.at[i, 6])
            drain(in0, ssem.at[i, 0])
            drain(in1.at[pl.ds(0, na - 1)], ssem.at[i, 1])
            drain(in2.at[pl.ds(0, nb - 1)], ssem.at[i, 2])
            drain(in3.at[pl.ds(0, nc - 1)], ssem.at[i, 3])
            drain(gb.at[pl.ds(0, (nb - 1) * n2)], ssem.at[i, 4])
            drain(ga.at[pl.ds(0, (na - 1) * n1)], ssem.at[i, 5])
            drain(in0, ssem.at[i, 6])

    held = {}

    def partner_a(k):
        onehots(p_src, pids, 4 * k, 512)
        onehots(p_dst.at[:, lanes[k]], pids, 16 + 4 * k, 512)
        h = dot(other_b[...], p_src[...])
        t = dot(own_b[...], p_dst[:, lanes[k]])
        q = complex_product(h, pr_s[:, lanes[k]])
        q_s[:, lanes[k]] = q
        g_pos = -jax.nn.sigmoid(-jnp.sum(q * t, axis=0, keepdims=True))
        for i, v in enumerate(split2(q * g_pos)):
            parts[400 * i : 400 * (i + 1), lanes[k]] = v

    def partner_b(k):
        q_b = q_s[:, lanes[k]].astype(bf16)
        gt[...] = (jax.nn.sigmoid(dot(own_b[...], q_b, 0, 0)) * 0.03125).astype(bf16)
        v = dot(q_b, gt[...], 1, 1) * counts(pids, 24 + 8 * k)
        dn[...] = v if k == 0 else dn[...] + v

    def dh(k):
        for i, v in enumerate(split2(conj_product(dq_s[:, lanes[k]], r_s[:, lanes[k]]))):
            dr2[400 * i : 400 * (i + 1), lanes[k]] = v

    def ent_scatter(n):
        rows = slice(256 * n, 256 * (n + 1))
        g = add2(dot(dr2[...], oh_src[rows, :], 1, 1) + dot(parts[...], p_dst[rows, :], 1, 1)) + dn[:, rows]
        for j in range(2):
            grad[2 * n + j] = g[:, 128 * j : 128 * (j + 1)].reshape(50, 8, 128)

    def ent(level):
        def push(src, dst, device):
            remote(src, dst, esend.at[level], erecv.at[level], device).start()

        if level == 0:
            for k in range(2):
                push(grad.at[2 * k + 1 - c], e0.at[k], near)
        elif level == 1:
            drain(e0, erecv.at[0])
            for k in range(2):
                hsum[k] = grad[2 * k + c] + e0[k]
            push(hsum.at[1 - zl], e1, far)
        elif level == 2:
            drain(e1, erecv.at[1])
            g = hsum[zl] + e1[...]
            square = jnp.sum(jnp.sum(g * g, axis=0), axis=0, keepdims=True)
            new_acc = acc[:, mine] + square * (1.0 / 400.0)
            nblk[m, 0:50] = emb[:, mine].reshape(50, 8, 128) - g * (learn_rate / jnp.sqrt(new_acc))
            nblk[m, 50] = jnp.broadcast_to(new_acc, (8, 128))
            push(nblk.at[m], nblk.at[m], far)
        elif level == 3:
            push(nblk.at[m], nblk.at[m], near)
        elif level == 4:
            drain(nblk.at[m], erecv.at[2])
            push(nblk.at[far_m], nblk.at[far_m], near)
        elif level == 5:
            drain(nblk.at[m], erecv.at[3])
            drain(nblk.at[m], erecv.at[4])
            for k in range(4):
                emb[:, 128 * k : 128 * (k + 1)] = nblk[k, 0:50].reshape(400, 128)
                acc[:, 128 * k : 128 * (k + 1)] = nblk[k, 50, 0:1]
            pltpu.make_async_copy(emb, nemb_out, osem.at[len(STREAMS)]).start()
            pltpu.make_async_copy(acc, nacc_out, osem.at[len(STREAMS) + 1]).start()
        else:
            drain(emb, osem.at[len(STREAMS)])
            drain(acc, osem.at[len(STREAMS) + 1])
            drain(e0, esend.at[0])
            drain(e1, esend.at[1])
            for k in range(2, 5):
                drain(nblk.at[m], esend.at[k])

    rel_scatter(0)
    rel_scatter(1)
    step(0, 0)
    rel_scatter(2)
    step(1, 0)
    step(0, 1)
    rel_scatter(3)
    step(2, 0)
    step(1, 1)
    step(2, 1)
    inputs[5].wait()
    partner_a(0)
    partner_b(0)
    partner_a(1)
    step(0, 2)
    partner_b(1)
    step(1, 2)
    step(2, 2)
    dh(0)
    dh(1)
    ent_scatter(0)
    ent_scatter(1)
    ent(0)
    step(0, 3)
    step(1, 3)
    step(2, 3)
    ent(1)
    step(0, 4)
    step(1, 4)
    step(2, 4)
    ent(2)
    ent(3)
    step(0, 5)
    step(2, 5)
    step(1, 5)
    ent(4)
    step(0, 6)
    step(2, 6)
    ent(5)
    step(1, 6)
    for i in range(3):
        step(i, 7)
    ent(6)

    for copy in (a_far, a_near, a_fwd):
        copy.wait_send()
    drain(pay, send1)

    @pl.when(is_hub)
    def _():
        drain(stage, send2)


def bucket_round(*args):
    tile = lambda *lead: pltpu.VMEM((*lead, 16, 128), bf16)
    t = lambda *lead: pltpu.VMEM((*lead, 8, 128), f32)
    V = pltpu.VMEM
    dma = pltpu.SemaphoreType.DMA
    scratch = [
        V((1, 1024), i32), V((1, 1024), i32), V((1, 1024), i32), V((1, 2, 1024), i32), V((400, 512), f32),
        V((1, 512), f32), V((400, 1024), f32), dma((7,)),
        tile(32), tile(2, 64), tile(64), tile(32), tile(4, 25), t(4, 51),
        dma, dma, dma, dma, dma, dma, dma((3,)), dma((3,)),
        V((40, 128), i32), V((40, 128), i32), V((400, 512), bf16), V((400, 512), bf16), V((1200, 1024), bf16),
        V((512, 1024), bf16), V((512, 1024), bf16), V((1024, 1024), bf16),
        V((512, 512), bf16), V((512, 1024), bf16), V((1024, 512), bf16),
        V((400, 1024), f32), V((400, 1024), f32), V((400, 1024), f32), V((400, 1024), bf16), V((400, 1024), f32),
        V((400, 1024), f32), V((400, 1024), f32), V((8, 512), f32),
        V((800, 1024), bf16), V((800, 1024), bf16), V((512, 512), bf16), V((400, 512), f32),
        t(2, 200), t(4, 50),
        t(2, 50), t(50), t(2, 50), dma((5,)), dma((5,)), dma((len(STREAMS), 7)), dma((len(STREAMS), 7)), dma((len(STREAMS) + 2,)),
    ]
    for _, n, axes in STREAMS:
        scratch += stream_scratch(25 * n, axes)
    return pl.pallas_call(
        round_kernel,
        out_shape=(
            jax.ShapeDtypeStruct((2, 200, 8, 128), f32),
            jax.ShapeDtypeStruct((400, 512), f32),
            jax.ShapeDtypeStruct((1, 512), f32),
        ),
        in_specs=[ANY] * 7 + [SMEM] * 2,
        out_specs=(ANY, ANY, ANY),
        scratch_shapes=scratch,
        compiler_params=pltpu.CompilerParams(
            collective_id=1, has_side_effects=True, vmem_limit_bytes=56 * 2**20
        ),
        name="bucket_round",
    )(*args)


def update_kernel(
    total, nemb, nacc, rel_in, racc_in, nemb_out, nacc_out, nrel_out, nracc_out, g_v, rel_v, racc_v, emb_v, acc_v, sem
):
    copies = []

    def move(src, dst):
        copies.append(pltpu.make_async_copy(src, dst, sem.at[len(copies)]))
        copies[-1].start()
        return copies[-1]

    rows = [slice(0, 200), slice(200, 400)]
    fetch_ent = [move(nemb, emb_v), move(nacc, acc_v)]
    fetch_g = [move(total.at[half], g_v.at[half]) for half in range(2)]
    fetch_racc = move(racc_in, racc_v)
    fetch_rel = [move(rel_in.at[rows[half]], rel_v.at[rows[half]]) for half in range(2)]
    leave = []
    for copy, src, dst in zip(fetch_ent, (emb_v, acc_v), (nemb_out, nacc_out)):
        copy.wait()
        leave.append(move(src, dst))
    squares = [jnp.zeros((8, 128), f32)] * 8
    for half in range(2):
        fetch_g[half].wait()
        for k in range(8):
            for i in range(25):
                v = g_v[half, 25 * k + i]
                squares[k] = squares[k] + v * v
    fetch_racc.wait()
    rates = []
    for k in range(8):
        lanes = slice(128 * k, 128 * (k + 1))
        new_racc = racc_v[:, lanes] + jnp.sum(squares[k], axis=0, keepdims=True) * (1.0 / 400.0)
        rates.append(learn_rate / jnp.sqrt(new_racc))
        racc_v[:, lanes] = new_racc
    leave.append(move(racc_v, nracc_out))
    for half in range(2):
        fetch_rel[half].wait()
        for k in range(8):
            lanes = slice(128 * k, 128 * (k + 1))
            g = g_v[half, 25 * k : 25 * (k + 1)].reshape(200, 128)
            rel_v[rows[half], lanes] = rel_v[rows[half], lanes] - g * rates[k]
        leave.append(move(rel_v.at[rows[half]], nrel_out.at[rows[half]]))
    for copy in leave:
        copy.wait()


def update(total, nemb, nacc, relations, racc):
    shape = lambda *s: jax.ShapeDtypeStruct(s, f32)
    V = pltpu.VMEM
    return pl.pallas_call(
        update_kernel,
        out_shape=(shape(400, 512), shape(1, 512), shape(400, 1024), shape(1, 1024)),
        in_specs=[ANY] * 5,
        out_specs=(ANY,) * 4,
        scratch_shapes=[
            V((2, 200, 8, 128), f32), V((400, 1024), f32), V((1, 1024), f32),
            V((400, 512), f32), V((1, 512), f32), pltpu.SemaphoreType.DMA((12,)),
        ],
        compiler_params=pltpu.CompilerParams(vmem_limit_bytes=60 * 2**20),
        name="update",
    )(total, nemb, nacc, relations, racc)


def shards(embeddings, accum, relations, rel_accum, src_ids, rel_ids, dst_ids, neg_ids, bucket_len, partner):
    total, nemb, nacc = bucket_round(
        src_ids, rel_ids, dst_ids, neg_ids, embeddings, accum.reshape(1, 512), relations, bucket_len, partner
    )
    new_emb, new_acc, new_rel, new_racc = update(total, nemb, nacc, relations, rel_accum.reshape(1, 1024))
    return new_emb, new_acc.reshape(512), new_rel, new_racc.reshape(1024)


def solution(mesh):
    return jax.shard_map(
        shards,
        mesh=mesh,
        in_specs=(
            P(None, "dom"), P("dom"), P(), P(), P("dom", "edge"), P("dom", "edge"), P("dom", "edge"),
            P("dom", "edge", None), P("dom"), P(),
        ),
        out_specs=(P(None, "dom"), P("dom"), P(), P()),
        check_vma=False,
    )
```
